128 devices in a mesh: group: 4 (over x), tile: 32 (over y, z, core).
Axes of the slice: x: 4, y: 4, z: 4, core: 2. Of those that a mesh axis runs over, the one named last changes fastest.
Arguments:
- velocity_u: float32 [4, 4096, 1024], P('group', 'tile'), may hold values from -6 to 6
- velocity_v: float32 [4, 4096, 1024], P('group', 'tile'), may hold values from -6 to 6
- tracer: float32 [4, 4096, 1024], P('group', 'tile'), may hold values from -6 to 6
- land: int32 [4096, 1024], P('tile'), may hold values 0 or 1
- tile_depth: int32 [256], replicated, may hold values from 1 to 4, 384 in all
- conv_one: bfloat16 [64, 3, 3, 3], replicated, may hold values from -1.25 to 1.25
- bias_one: float32 [64], replicated, may hold values from -3 to 3
- conv_two: bfloat16 [64, 64, 3, 3], replicated, may hold values from -0.25 to 0.25
- bias_two: float32 [64], replicated, may hold values from -3 to 3
- conv_three: bfloat16 [3, 64, 3, 3], replicated, may hold values from -0.25 to 0.25
- bias_three: float32 [3], replicated, may hold values from -3 to 3
Outputs:
- east_two: float32 [4, 4096, 1024], P('group', 'tile')
- north_two: float32 [4, 4096, 1024], P('group', 'tile')
- tracer_one: float32 [4, 4096, 1024], P('group', 'tile')
The draws below stay inside these ranges and needn't reach their ends.
Inputs may be any that keep to these rules, and one draw needn't show every extreme that they name: `land`: 1 marks water. `tile_depth`: the entries sum to exactly 384; some column is 4 levels deep.
All inputs are finite; a program needn't handle non-finite values. No bound on the sum of `land` on one device may be relied on, other than what follows from the above.
Results may differ from the reference program's by a relative error of at most 0.00083.
Values may be sent and summed in bfloat16 or wider, within the bound.
A program may use at most 128 MiB of HBM per device.

```python
import math
import jax
import jax.numpy as jnp
import numpy as np
from jax import lax

TS = 128
NTY = 8
CH = 64
C_IN = 3
C_OUT = 3
WET_DEV = 3
LEV = 4
NX = 4096
NY = 1024
NTILES = 256
WET_TILES = 384
N_GROUP = 4
N_TILE = 32


def place_ends(drawn, key, low, largest):
    shape = drawn.shape
    spot = [jax.random.randint(jax.random.fold_in(key, axis), (), 0, shape[axis]) for axis in range(len(shape))]
    drawn = drawn.at[tuple(spot)].set(low)
    longest = shape.index(max(shape))
    spot[longest] = (spot[longest] + 1) % shape[longest]
    return drawn.at[tuple(spot)].set(largest)


def block_levels(stream_key, dims, pieces, least, largest):
    def one(dim, shards_of):
        heights = jax.random.uniform(jax.random.fold_in(jax.random.fold_in(stream_key, 6), dim), (shards_of,), jnp.float32, least / len(pieces), largest / len(pieces))
        return jnp.repeat(jnp.exp(heights), dims[dim] // shards_of).reshape((-1,) + (1,) * (len(dims) - dim - 1))

    gain = one(*pieces[0])
    for cut in pieces[1:]:
        gain = gain * one(*cut)
    return gain


def length_profile(amount, total, most, skew):
    loads = [(1 << 20) // math.isqrt(standing ** skew) + 1 for standing in range(2, amount + 1)]
    spare, holding = total - most - (amount - 1), [1] * (amount - 1)
    while spare > 0:
        free = [i for i in range(amount - 1) if holding[i] < most]
        mass, budget = sum([loads[i] for i in free]), spare
        for i in free:
            more = min(most - holding[i], max(1, budget * loads[i] // mass), spare)
            holding[i] = holding[i] + more
            spare = spare - more
    return np.array([most] + holding)


def uneven_parts(stream_key, number_of, total, bound, slope):
    if number_of == 2:
        one = jax.random.randint(stream_key, (), max(1, total - bound), min(bound, total - 1) + 1)
        return jnp.stack([one, total - one])
    tallies = jnp.asarray(length_profile(number_of, total, bound, slope), jnp.int32)
    couples = (number_of - 1) // 2
    donor, receiver = tallies[1:1 + 2 * couples:2], tallies[2:2 + 2 * couples:2]
    room = jnp.minimum(donor - 1, bound - receiver)
    shifted = jax.random.randint(jax.random.fold_in(stream_key, 1), (couples,), 0, 1 << 20) % (room + 1)
    tallies = tallies.at[1:1 + 2 * couples:2].set(donor - shifted).at[2:2 + 2 * couples:2].set(receiver + shifted)
    return tallies[jax.random.permutation(jax.random.fold_in(stream_key, 2), number_of)]


def bell_draw(own_key, dims, width, most, split=(), held_as=jnp.bfloat16):
    factor_of = block_levels(own_key, dims, split, -0.22, 0.18) if split else 1.0
    values = jax.random.normal(own_key, dims, jnp.float32) * width * factor_of
    return jnp.minimum(jnp.maximum(values, -most), most).astype(held_as)


def setup_inputs(seed: int = 0) -> dict:
    streams_of = jax.random.split(jax.random.key(seed), 12)
    velocity_u = bell_draw(streams_of[0], (LEV, NX, NY), 1.0, 6.0, ((0, 4), (1, 32)), jnp.float32)
    velocity_v = bell_draw(streams_of[1], (LEV, NX, NY), 1.0, 6.0, ((0, 4), (1, 32)), jnp.float32)
    tracer = bell_draw(streams_of[2], (LEV, NX, NY), 1.0, 6.0, ((0, 4), (1, 32)), jnp.float32)
    land = place_ends((jax.random.randint(streams_of[3], (NX, NY), 0, 8) < 7).astype(jnp.int32), jax.random.fold_in(streams_of[3], 1), 0, 1)
    tile_depth = uneven_parts(streams_of[4], NTILES, WET_TILES, LEV, 2).astype(jnp.int32)
    conv_one = bell_draw(streams_of[5], (CH, C_IN, 3, 3), (C_IN * 9) ** -0.5, 1.25)
    bias_one = bell_draw(streams_of[6], (CH,), 0.5, 3.0, (), jnp.float32)
    conv_two = bell_draw(streams_of[7], (CH, CH, 3, 3), (CH * 9) ** -0.5, 0.25)
    bias_two = bell_draw(streams_of[8], (CH,), 0.5, 3.0, (), jnp.float32)
    conv_three = bell_draw(streams_of[9], (C_OUT, CH, 3, 3), (CH * 9) ** -0.5, 0.25)
    bias_three = bell_draw(streams_of[10], (C_OUT,), 0.5, 3.0, (), jnp.float32)
    return dict(velocity_u=velocity_u, velocity_v=velocity_v, tracer=tracer, land=land, tile_depth=tile_depth, conv_one=conv_one, bias_one=bias_one, conv_two=conv_two, bias_two=bias_two, conv_three=conv_three, bias_three=bias_three)


time_step = 0.1
viscosity = 0.5
diffusivity = 0.5
eddy_gain = 0.5
coriolis_base = 0.2
coriolis_slope = 0.6


def east_diff(field):
    return 0.5 * (field[..., 2:, 1:-1] - field[..., :-2, 1:-1])


def north_diff(field):
    return 0.5 * (field[..., 1:-1, 2:] - field[..., 1:-1, :-2])


def laplace(field):
    return (field[..., 2:, 1:-1] + field[..., :-2, 1:-1] + field[..., 1:-1, 2:]
            + field[..., 1:-1, :-2] - 4.0 * field[..., 1:-1, 1:-1])


def advance(padded_east, padded_north, padded_tracer, active, coriolis):
    inner_east = padded_east[..., 1:-1, 1:-1]
    inner_north = padded_north[..., 1:-1, 1:-1]
    inner_tracer = padded_tracer[..., 1:-1, 1:-1]
    grad_east = east_diff(padded_tracer)
    grad_north = north_diff(padded_tracer)
    new_east = inner_east + time_step * active * (coriolis * inner_north - grad_east + viscosity * laplace(padded_east))
    new_north = inner_north + time_step * active * (-coriolis * inner_east - grad_north + viscosity * laplace(padded_north))
    new_tracer = inner_tracer + time_step * active * (-(inner_east * grad_east + inner_north * grad_north) + diffusivity * laplace(padded_tracer))
    return new_east, new_north, new_tracer


def convolve(source, kernel):
    return lax.conv_general_dilated(source.astype(jnp.float32), kernel.astype(jnp.float32), (1, 1), "VALID",
                                    dimension_numbers=("NCHW", "OIHW", "NCHW"), precision=lax.Precision.HIGHEST)


def closure(window, conv_one, bias_one, conv_two, bias_two, conv_three, bias_three):
    hidden_one = jax.nn.silu(convolve(window, conv_one) + bias_one[None, :, None, None]).astype(jnp.bfloat16)
    hidden_two = jax.nn.silu(convolve(hidden_one, conv_two) + bias_two[None, :, None, None]).astype(jnp.bfloat16)
    return (convolve(hidden_two, conv_three) + bias_three[None, :, None, None]).astype(jnp.bfloat16)


def reference(velocity_u, velocity_v, tracer, land, tile_depth, conv_one, bias_one, conv_two, bias_two, conv_three, bias_three):
    depth_grid = tile_depth.reshape(N_TILE, NTY)
    depth_cells = jnp.repeat(jnp.repeat(depth_grid, TS, axis=0), TS, axis=1)
    levels = jnp.arange(LEV, dtype=jnp.int32)
    active = ((land[None] == 1) & (levels[:, None, None] < depth_cells[None])).astype(jnp.float32)
    coriolis = (coriolis_base + coriolis_slope * (jnp.arange(NX, dtype=jnp.float32) + 0.5) / NX)[:, None]
    padded = jnp.pad(jnp.stack([velocity_u, velocity_v, tracer]), ((0, 0), (0, 0), (1, 1), (1, 1)))
    east_one, north_one, tracer_one = advance(padded[0], padded[1], padded[2], active, coriolis)
    features = (jnp.stack([east_one, north_one, tracer_one], axis=1) * active[:, None]).astype(jnp.bfloat16)
    framed = jnp.pad(features, ((0, 0), (0, 0), (3, 3), (3, 3)))
    wet_flags = (levels[:, None, None] < depth_grid[None]).astype(jnp.int32)
    order = jnp.argsort(1 - wet_flags.reshape(-1), stable=True)[: WET_DEV * N_GROUP * N_TILE].astype(jnp.int32)
    tiles_all = LEV * N_TILE * NTY

    def one_tile(index):
        level = index // (N_TILE * NTY)
        place = index % (N_TILE * NTY)
        row_tile = place // NTY
        col_tile = place % NTY
        window = lax.dynamic_slice(framed, (level, jnp.int32(0), row_tile * TS, col_tile * TS), (1, C_IN, TS + 6, TS + 6))
        return closure(window, conv_one, bias_one, conv_two, bias_two, conv_three, bias_three)[0]

    stresses = lax.map(one_tile, order)
    placed = jnp.zeros((tiles_all, C_OUT, TS, TS), jnp.bfloat16).at[order].set(stresses)
    stress = placed.reshape(LEV, N_TILE, NTY, C_OUT, TS, TS).transpose(0, 3, 1, 4, 2, 5).reshape(LEV, C_OUT, NX, NY)
    masked = (stress.astype(jnp.float32) * active[:, None]).astype(jnp.bfloat16)
    framed_stress = jnp.pad(masked.astype(jnp.float32), ((0, 0), (0, 0), (1, 1), (1, 1)))
    push_east = east_diff(framed_stress[:, 0]) + north_diff(framed_stress[:, 1])
    push_north = east_diff(framed_stress[:, 1]) + north_diff(framed_stress[:, 2])
    east_two = east_one + eddy_gain * active * push_east
    north_two = north_one + eddy_gain * active * push_north
    return east_two, north_two, tracer_one
```

```python
import functools

import jax
import jax.numpy as jnp
import numpy as np
from jax import lax
from jax.experimental import pallas as pl
from jax.experimental.pallas import tpu as pltpu
from jax.sharding import PartitionSpec as P

time_step = 0.1
viscosity = 0.5
diffusivity = 0.5
eddy_gain = 0.5
coriolis_base = 0.2
coriolis_slope = 0.6

bf16 = jnp.bfloat16
f32 = jnp.float32

TS = 128
HALO = 5
ROWS1, ROWS2, ROWS3 = 35, 34, 33
SLAB = 160
USED = 144


def select_in():
    table = np.zeros((80, 256), np.float32)
    for t in range(10):
        for s in range(8):
            table[t * 8 + s, 2 * (9 * s + t)] = 1.0
    return table


def select_out():
    table = np.zeros((2, 2, 160, 256), np.float32)
    for ip in range(2):
        for b in range(2):
            for t in range(9):
                for s in range(8):
                    place = 2 * (9 * s + t) + b
                    if place < 130:
                        table[ip, b, t * 16 + ip * 8 + s, place] = 1.0
    return table


def taps():
    for outer in range(2):
        for inner in range(2):
            for out in range(2):
                k = 2 * outer + inner - out
                if 0 <= k < 3:
                    yield outer, inner, out, k


def build_weights(w1, w2, w3, w1f, w1s, w2s, w3f, w3s):
    w1f[...] = jnp.zeros_like(w1f)
    for q in range(4):
        for dj, dy, b, ky in taps():
            for c in range(3):
                for a in range(2):
                    row = dj * 128 + dy * 48 + c * 16 + 4 + 2 * q + a
                    lane = (a * 2 + b) * 64
                    w1f[q, row : row + 3, lane : lane + 64] = 0.5 * w1[c, ky]
    w1s[...] = w1f[...].astype(bf16)
    w2s[...] = jnp.zeros_like(w2s)
    for di, ai, ao, kx in taps():
        for dj, bi, bo, ky in taps():
            row = (ai * 2 + bi) * 64
            lane = (ao * 2 + bo) * 64
            w2s[di * 2 + dj, row : row + 64, lane : lane + 64] = (0.5 * w2[kx, ky]).astype(bf16)
    w3f[...] = jnp.zeros_like(w3f)
    for di, ai, ao, kx in taps():
        for dj, bi, bo, ky in taps():
            lane = (ai * 2 + bi) * 64
            for c in range(3):
                row = (di * 2 + dj) * 16 + bo * 6 + c * 2 + ao
                w3f[row : row + 1, lane : lane + 64] = w3[c, kx, ky : ky + 1]
    w3s[...] = w3f[...].astype(bf16)


def build_features(meta, depth, u, v, t, land, lo, hi, east, north, tracer, ext, landx, feat, act):
    level, tile = meta[0], meta[1]
    cols = u.shape[1]
    for f, src in enumerate((u, v, t)):
        ext[f, 0:16, :] = jnp.zeros((16, cols), f32)
        ext[f, 144:160, :] = jnp.zeros((16, cols), f32)
        ext[f, 16:144, :] = src[...]
        ext[f, 16 - HALO : 16, :] = lo[f]
        ext[f, 144 : 144 + HALO, :] = hi[f]
    landx[0:16, :] = jnp.zeros((16, cols), f32)
    landx[144:160, :] = jnp.zeros((16, cols), f32)
    landx[16:144, :] = land[...].astype(f32)
    landx[16 - HALO : 16, :] = lo[3]
    landx[144 : 144 + HALO, :] = hi[3]
    lane = lax.broadcasted_iota(jnp.int32, (8, cols), 1)
    row = lax.broadcasted_iota(jnp.int32, (8, cols), 0)
    last = depth.shape[0] // (cols // TS) - 1

    def wet_line(tile_row):
        line = jnp.zeros((8, cols), f32)
        for ty in range(cols // TS):
            wet = (depth[tile_row * (cols // TS) + ty] > level).astype(f32)
            line = jnp.where(lane // TS == ty, wet, line)
        return line

    wet_low = wet_line(jnp.maximum(tile - 1, 0))
    wet_mid = wet_line(tile)
    wet_high = wet_line(jnp.minimum(tile + 1, last))
    rows_all = float((last + 1) * TS)
    zeros = jnp.zeros((8, TS), f32)

    def west(x):
        return jnp.where(lane == 0, 0.0, pltpu.roll(x, 1, 1))

    def east_of(x):
        return jnp.where(lane == cols - 1, 0.0, pltpu.roll(x, cols - 1, 1))

    for k in range(-1, 17):
        base = 8 * k + 16
        wet = wet_low if k < 0 else (wet_high if k > 15 else wet_mid)
        active = jnp.where(landx[base : base + 8, :] == 1.0, wet, 0.0)
        mid = [ext[f, base : base + 8, :] for f in range(3)]
        up = [ext[f, base - 1 : base + 7, :] for f in range(3)]
        down = [ext[f, base + 1 : base + 9, :] for f in range(3)]
        left = [west(x) for x in mid]
        right = [east_of(x) for x in mid]
        lap = [down[f] + up[f] + right[f] + left[f] - 4.0 * mid[f] for f in range(3)]
        grad_east = 0.5 * (down[2] - up[2])
        grad_north = 0.5 * (right[2] - left[2])
        place = (tile * TS + 8 * k + row).astype(f32)
        coriolis = coriolis_base + coriolis_slope * (place + 0.5) / rows_all
        step = time_step * active
        new_east = mid[0] + step * (coriolis * mid[1] - grad_east + viscosity * lap[0])
        new_north = mid[1] + step * (-coriolis * mid[0] - grad_north + viscosity * lap[1])
        new_tracer = mid[2] + step * (
            -(mid[0] * grad_east + mid[1] * grad_north) + diffusivity * lap[2]
        )
        if 0 <= k < 16:
            east[8 * k : 8 * k + 8, :] = new_east
            north[8 * k : 8 * k + 8, :] = new_north
            tracer[8 * k : 8 * k + 8, :] = new_tracer
        q = 8 * k + 8
        for c, new in enumerate((new_east, new_north, new_tracer)):
            wide = jnp.concatenate([new * active, zeros], axis=1)
            feat[0, c, q : q + 8, :] = pltpu.roll(wide, 4, 1)
            feat[1, c, q : q + 8, :] = pltpu.roll(wide, 3, 1)
        act[q : q + 8, :] = pltpu.roll(jnp.concatenate([active, zeros], axis=1), 1, 1)


def silu_half(half):
    return half + half * jnp.tanh(half)


def store_slab(ref, index, value):
    ref[index, 0:USED, :] = value.astype(bf16)
    ref[index, USED:SLAB, :] = pltpu.roll(value[0:16], 15, 0).astype(bf16)


def closure_tile(lane0, sel_in, sel_out, b1, b2, b3, w1s, w2s, w3s, feat, patches, h1, h2, parts, flat):
    for g in range(9):
        halves = []
        for ip in range(2):
            base = 64 * ip + 8 * g
            rows = feat[:, :, base : base + 16, pl.ds(lane0, 256)].reshape(96, 256)
            rows = jnp.concatenate([rows, jnp.zeros((32, 256), f32)], axis=0).astype(bf16)
            got = lax.dot_general(
                sel_in[...], rows, (((1,), (1,)), ((), ())), preferred_element_type=f32
            )
            halves.append(got.reshape(10, 8, 128))
        both = jnp.stack(halves, axis=1).reshape(SLAB, 128)
        patches[g] = both.astype(bf16)
    for q in range(4):
        for g in range(9):
            if 4 * g + q >= ROWS1:
                continue
            lhs = jnp.concatenate([patches[g, 0:USED, :], patches[g, 16:SLAB, :]], axis=1)
            half = jnp.dot(lhs, w1s[q], preferred_element_type=f32) + b1[...]
            store_slab(h1, 4 * g + q, silu_half(half))
    for i in range(0, ROWS2, 2):
        half = b2[...]
        for di in range(2):
            for dj in range(2):
                lhs = h1[i + di : i + di + 2, 16 * dj : 16 * dj + USED, :].reshape(2 * USED, 256)
                half = half + jnp.dot(lhs, w2s[2 * di + dj], preferred_element_type=f32)
        out = silu_half(half)
        store_slab(h2, i, out[0:USED])
        store_slab(h2, i + 1, out[USED:])
    for i in range(ROWS2):
        parts[i] = lax.dot_general(
            w3s[...], h2[i], (((1,), (1,)), ((), ())), preferred_element_type=f32
        )
    for i in range(ROWS3):
        got = (
            parts[i, 0:16, 0:USED]
            + parts[i, 16:32, 16:SLAB]
            + parts[i + 1, 32:48, 0:USED]
            + parts[i + 1, 48:64, 16:SLAB]
        )
        for b in range(2):
            for c in range(3):
                r = b * 6 + c * 2
                flat[b, c, 2 * i : 2 * i + 2, 0:USED] = got[r : r + 2] + b3[c]


def finish_tile(lane0, sel_out, flat, act, east, north):
    for ip in range(2):
        mask = act[8 + 64 * ip - 1 : 8 + 64 * ip + 65, pl.ds(lane0, 256)]
        masked = []
        for c in range(3):
            image = jnp.zeros((72, 256), f32)
            for b in range(2):
                image = image + jnp.dot(
                    flat[b, c].astype(bf16), sel_out[ip, b], preferred_element_type=f32
                )
            masked.append(image[0:66] * mask)
        xx, xy, yy = masked

        def dx(m):
            return 0.5 * (m[2:66, 1:129] - m[0:64, 1:129])

        def dy(m):
            return 0.5 * (m[1:65, 2:130] - m[1:65, 0:128])

        gain = eddy_gain * mask[1:65, 1:129]
        rows = slice(64 * ip, 64 * ip + 64)
        east[rows, pl.ds(lane0, 128)] += gain * (dx(xx) + dy(xy))
        north[rows, pl.ds(lane0, 128)] += gain * (dx(xy) + dy(yy))


def kernel(
    meta, depth, b3, u, v, t, land, lo, hi, w1, b1, w2, b2, w3, sel_in, sel_out,
    east, north, tracer,
    ext, landx, feat, act, w1f, w1s, w2s, w3f, w3s, patches, h1, h2, parts, flat,
):
    build_weights(w1, w2, w3, w1f, w1s, w2s, w3f, w3s)
    build_features(meta, depth, u, v, t, land, lo, hi, east, north, tracer, ext, landx, feat, act)
    flat[...] = jnp.zeros_like(flat)
    across = u.shape[1] // TS

    def column(ty, carry):
        @pl.when(depth[meta[1] * across + ty] > meta[0])
        def _():
            lane0 = pl.multiple_of(ty * TS, TS)
            closure_tile(
                lane0, sel_in, sel_out, b1, b2, b3, w1s, w2s, w3s, feat, patches, h1, h2, parts, flat
            )
            finish_tile(lane0, sel_out, flat, act, east, north)

        return carry

    lax.fori_loop(0, across, column, 0)


def body(u, v, t, land, depth, conv_one, bias_one, conv_two, bias_two, conv_three, bias_three):
    levels, rows, cols = u.shape
    tiles = lax.axis_size("tile")
    fields = jnp.concatenate([u, v, t, land[None].astype(f32)], axis=0)
    forward = [(i, i + 1) for i in range(tiles - 1)]
    backward = [(i + 1, i) for i in range(tiles - 1)]
    lo = lax.ppermute(fields[:, rows - HALO :], "tile", forward)
    hi = lax.ppermute(fields[:, :HALO], "tile", backward)
    meta = jnp.stack([lax.axis_index("group"), lax.axis_index("tile")]).astype(jnp.int32)
    w1 = conv_one.transpose(1, 3, 2, 0).astype(f32)
    w2 = conv_two.transpose(2, 3, 1, 0).astype(f32)
    w3 = conv_three.transpose(0, 2, 3, 1).astype(f32)
    b1 = jnp.tile(0.5 * bias_one, 4)[None]
    b2 = jnp.tile(0.5 * bias_two, 4)[None]
    sel_in = jnp.asarray(select_in(), bf16)
    sel_out = jnp.asarray(select_out(), bf16)
    vmem = pl.BlockSpec(memory_space=pltpu.VMEM)
    smem = pl.BlockSpec(memory_space=pltpu.SMEM)
    wide = cols + TS
    east, north, tracer = pl.pallas_call(
        kernel,
        out_shape=[jax.ShapeDtypeStruct((rows, cols), f32)] * 3,
        in_specs=[smem] * 3 + [vmem] * 13,
        out_specs=[vmem] * 3,
        scratch_shapes=[
            pltpu.VMEM((3, 160, cols), f32),
            pltpu.VMEM((160, cols), f32),
            pltpu.VMEM((2, 3, 144, wide), f32),
            pltpu.VMEM((144, wide), f32),
            pltpu.VMEM((4, 256, 256), f32),
            pltpu.VMEM((4, 256, 256), bf16),
            pltpu.VMEM((4, 256, 256), bf16),
            pltpu.VMEM((64, 256), f32),
            pltpu.VMEM((64, 256), bf16),
            pltpu.VMEM((9, SLAB, 128), bf16),
            pltpu.VMEM((ROWS1 + 1, SLAB, 256), bf16),
            pltpu.VMEM((ROWS2, SLAB, 256), bf16),
            pltpu.VMEM((ROWS2, 64, SLAB), f32),
            pltpu.VMEM((2, 3, 72, SLAB), f32),
        ],
        compiler_params=pltpu.CompilerParams(vmem_limit_bytes=56 * 2**20),
        name="step",
    )(meta, depth, bias_three, u[0], v[0], t[0], land, lo, hi, w1, b1, w2, b2, w3, sel_in, sel_out)
    return east[None], north[None], tracer[None]


def solution(mesh):
    field = P("group", "tile", None)
    in_specs = (field, field, field, P("tile", None)) + (P(),) * 7
    return jax.shard_map(
        body, mesh=mesh, in_specs=in_specs, out_specs=(field,) * 3, check_vma=False
    )
```

```python
import jax
import jax.numpy as jnp
import numpy as np
from jax import lax
from jax.experimental import pallas as pl
from jax.experimental.pallas import tpu as pltpu
from jax.sharding import PartitionSpec as P

time_step = 0.1
viscosity = 0.5
diffusivity = 0.5
eddy_gain = 0.5
coriolis_base = 0.2
coriolis_slope = 0.6

bf16 = jnp.bfloat16
f32 = jnp.float32

TS = 128
HALO = 5
ROWS1, ROWS2, ROWS3 = 35, 34, 33
SLAB = 160
USED = 144


def select_in():
    table = np.zeros((80, 256), np.float32)
    for t in range(10):
        for s in range(8):
            table[t * 8 + s, 2 * (9 * s + t)] = 1.0
    return table


def select_out():
    table = np.zeros((2, 2, 160, 256), np.float32)
    for ip in range(2):
        for b in range(2):
            for t in range(9):
                for s in range(8):
                    place = 2 * (9 * s + t) + b
                    if place < 130:
                        table[ip, b, t * 16 + ip * 8 + s, place] = 1.0
    return table


def taps():
    for outer in range(2):
        for inner in range(2):
            for out in range(2):
                k = 2 * outer + inner - out
                if 0 <= k < 3:
                    yield outer, inner, out, k


def build_weights(w1, w2, w3, w1f, w1s, w2s, w3f, w3s):
    w1f[...] = jnp.zeros_like(w1f)
    for q in range(4):
        for dj, dy, b, ky in taps():
            for c in range(3):
                for a in range(2):
                    row = dj * 128 + dy * 48 + c * 16 + 4 + 2 * q + a
                    lane = (a * 2 + b) * 64
                    w1f[q, row : row + 3, lane : lane + 64] = 0.5 * w1[c, ky]
    w1s[...] = w1f[...].astype(bf16)
    w2s[...] = jnp.zeros_like(w2s)
    for di, ai, ao, kx in taps():
        for dj, bi, bo, ky in taps():
            row = (ai * 2 + bi) * 64
            lane = (ao * 2 + bo) * 64
            w2s[di * 2 + dj, row : row + 64, lane : lane + 64] = (0.5 * w2[kx, ky]).astype(bf16)
    w3f[...] = jnp.zeros_like(w3f)
    for di, ai, ao, kx in taps():
        for dj, bi, bo, ky in taps():
            lane = (ai * 2 + bi) * 64
            for c in range(3):
                row = (di * 2 + dj) * 16 + bo * 6 + c * 2 + ao
                w3f[row : row + 1, lane : lane + 64] = w3[c, kx, ky : ky + 1]
    w3s[...] = w3f[...].astype(bf16)


def wet_line(depth, level, tile_row, lane, across):
    line = jnp.zeros(lane.shape, f32)
    for ty in range(across):
        wet = (depth[tile_row * across + ty] > level).astype(f32)
        line = jnp.where(lane // TS == ty, wet, line)
    return line


def feature_rows(k, tile, rows_all, wet, ext, landx, east, north, tracer, feat, act, act0, store):
    cols = landx.shape[1]
    lane = lax.broadcasted_iota(jnp.int32, (8, cols), 1)
    row = lax.broadcasted_iota(jnp.int32, (8, cols), 0)
    zeros = jnp.zeros((8, TS), f32)

    def west(x):
        return jnp.where(lane == 0, 0.0, pltpu.roll(x, 1, 1))

    def east_of(x):
        return jnp.where(lane == cols - 1, 0.0, pltpu.roll(x, cols - 1, 1))

    base = 8 * k + 16
    if not isinstance(k, int):
        base = pl.multiple_of(base, 8)
    water = jnp.where(landx[pl.ds(base, 8), :] == 1, 1.0, 0.0)
    active = water * wet
    above = base - 8 if isinstance(k, int) else pl.multiple_of(base - 8, 8)
    around = [ext[f, pl.ds(above, 24), :] for f in range(3)]
    mid = [x[8:16] for x in around]
    up = [x[7:15] for x in around]
    down = [x[9:17] for x in around]
    left = [west(x) for x in mid]
    right = [east_of(x) for x in mid]
    lap = [down[f] + up[f] + right[f] + left[f] - 4.0 * mid[f] for f in range(3)]
    grad_east = 0.5 * (down[2] - up[2])
    grad_north = 0.5 * (right[2] - left[2])
    place = (tile * TS + 8 * k + row).astype(f32)
    coriolis = coriolis_base + coriolis_slope * (place + 0.5) / rows_all
    step = time_step * active
    new_east = mid[0] + step * (coriolis * mid[1] - grad_east + viscosity * lap[0])
    new_north = mid[1] + step * (-coriolis * mid[0] - grad_north + viscosity * lap[1])
    new_tracer = mid[2] + step * (
        -(mid[0] * grad_east + mid[1] * grad_north) + diffusivity * lap[2]
    )
    if store:
        at = 8 * k
        if not isinstance(k, int):
            at = pl.multiple_of(at, 8)
        east[pl.ds(at, 8), :] = new_east
        north[pl.ds(at, 8), :] = new_north
        tracer[pl.ds(at, 8), :] = new_tracer
    q = 8 * k + 8
    if not isinstance(k, int):
        q = pl.multiple_of(q, 8)
    for c, new in enumerate((new_east, new_north, new_tracer)):
        wide = jnp.concatenate([new * active, zeros], axis=1)
        feat[c, pl.ds(q, 8), :] = pltpu.roll(wide, 4, 1)
    act[pl.ds(q, 8), :] = pltpu.roll(jnp.concatenate([active, zeros], axis=1), 1, 1)
    act0[pl.ds(q, 8), :] = pltpu.roll(jnp.concatenate([water, zeros], axis=1), 1, 1)


def silu_half(half):
    return half + half * jnp.tanh(half)


def store_slab(ref, index, value):
    ref[index, 0:USED, :] = value.astype(bf16)
    ref[index, USED:SLAB, :] = pltpu.roll(value[0:16], 15, 0).astype(bf16)


def closure_tile(win, mwin, res, sel_in, sel_out, b1, b2, b3, w1s, w2s, w3s, patches, h1, h2, parts, flat):
    for g in range(9):
        halves = []
        for ip in range(2):
            base = 64 * ip + 8 * g
            rows = win[:, base : base + 16, :].reshape(48, 256)
            rows = jnp.concatenate([rows, pltpu.roll(rows, 255, 1), jnp.zeros((32, 256), f32)], axis=0)
            got = lax.dot_general(
                sel_in[...], rows.astype(bf16), (((1,), (1,)), ((), ())), preferred_element_type=f32
            )
            halves.append(got.reshape(10, 8, 128))
        patches[g] = jnp.stack(halves, axis=1).reshape(SLAB, 128).astype(bf16)
    for q in range(4):
        for g in range(9):
            if 4 * g + q >= ROWS1:
                continue
            lhs = jnp.concatenate([patches[g, 0:USED, :], patches[g, 16:SLAB, :]], axis=1)
            half = jnp.dot(lhs, w1s[q], preferred_element_type=f32) + b1[...]
            store_slab(h1, 4 * g + q, silu_half(half))
    for i in range(0, ROWS2, 2):
        half = b2[...]
        for di in range(2):
            for dj in range(2):
                lhs = h1[i + di : i + di + 2, 16 * dj : 16 * dj + USED, :].reshape(2 * USED, 256)
                half = half + jnp.dot(lhs, w2s[2 * di + dj], preferred_element_type=f32)
        out = silu_half(half)
        store_slab(h2, i, out[0:USED])
        store_slab(h2, i + 1, out[USED:])
    for i in range(ROWS2):
        parts[i] = lax.dot_general(
            w3s[...], h2[i], (((1,), (1,)), ((), ())), preferred_element_type=f32
        )
    for i in range(ROWS3):
        got = (
            parts[i, 0:16, 0:USED]
            + parts[i, 16:32, 16:SLAB]
            + parts[i + 1, 32:48, 0:USED]
            + parts[i + 1, 48:64, 16:SLAB]
        )
        for b in range(2):
            for c in range(3):
                r = b * 6 + c * 2
                flat[b, c, 2 * i : 2 * i + 2, 0:USED] = got[r : r + 2] + b3[c]
    for ip in range(2):
        mask = mwin[8 + 64 * ip - 1 : 8 + 64 * ip + 65, :]
        masked = []
        for c in range(3):
            image = jnp.zeros((72, 256), f32)
            for b in range(2):
                image = image + jnp.dot(
                    flat[b, c].astype(bf16), sel_out[ip, b], preferred_element_type=f32
                )
            masked.append(image[0:66] * mask)
        xx, xy, yy = masked

        def dx(m):
            return 0.5 * (m[2:66, 1:129] - m[0:64, 1:129])

        def dy(m):
            return 0.5 * (m[1:65, 2:130] - m[1:65, 0:128])

        gain = eddy_gain * mask[1:65, 1:129]
        rows = slice(64 * ip, 64 * ip + 64)
        res[0, rows, :] = gain * (dx(xx) + dy(xy))
        res[1, rows, :] = gain * (dx(xy) + dy(yy))


def add_push(east, north, res, lane0):
    east[:, pl.ds(lane0, TS)] += res[0]
    north[:, pl.ds(lane0, TS)] += res[1]


KEPT = 5


def first_kernel(
    depth, b3, u, v, t, land, w1, b1, w2, b2, w3, sel_in, sel_out, pick,
    east, north, tracer, feat_out, act_out, w1s, w2s, w3s,
    ext, landx, feat, act, act0, w1f, w3f, patches, h1, h2, parts, flat, win, mwin, res,
    main_out, edge_out, main_in, edge_in, res_out, res_in,
    halo_send, halo_recv, win_send, win_recv, res_send, res_recv,
):
    level, tile = lax.axis_index("group"), lax.axis_index("tile")
    tiles = lax.axis_size("tile")
    cols = u.shape[1]
    across = cols // TS
    mesh_id = pl.DeviceIdType.MESH

    barrier = pltpu.get_barrier_semaphore()

    def greet(group, place):
        pl.semaphore_signal(barrier, inc=1, device_id=(group, place), device_id_type=mesh_id)

    @pl.when(tile > 0)
    def _():
        greet(level, tile - 1)

    @pl.when(tile < tiles - 1)
    def _():
        greet(level, tile + 1)

    @pl.when(level == 0)
    def _():
        greet(2, tile)
        greet(3, tile)

    @pl.when(level >= 2)
    def _():
        greet(0, tile)

    peers = jnp.where(tile > 0, 1, 0) + jnp.where(tile < tiles - 1, 1, 0)
    peers = peers + jnp.where(level == 0, 2, jnp.where(level == 1, 0, 1))
    pl.semaphore_wait(barrier, peers)

    def halo_copy(way, f):
        src = (u, v, t, land)[f]
        rows_from, rows_to, place = ((TS - 8, 8, tile + 1), (0, 144, tile - 1))[way]
        dst = ext.at[f, pl.ds(rows_to, 8)] if f < 3 else landx.at[pl.ds(rows_to, 8)]
        return pltpu.make_async_remote_copy(
            src_ref=src.at[pl.ds(rows_from, 8)],
            dst_ref=dst,
            send_sem=halo_send.at[way, f],
            recv_sem=halo_recv.at[way, f],
            device_id=(level, place),
            device_id_type=mesh_id,
        )

    @pl.when(tile < tiles - 1)
    def _():
        for f in range(4):
            halo_copy(0, f).start()

    @pl.when(tile > 0)
    def _():
        for f in range(4):
            halo_copy(1, f).start()

    for f, src in enumerate((u, v, t)):
        ext[f, 0:8, :] = jnp.zeros((8, cols), f32)
        ext[f, 152:160, :] = jnp.zeros((8, cols), f32)
        ext[f, 16:144, :] = src[...]
    landx[0:8, :] = jnp.zeros((8, cols), jnp.int32)
    landx[152:160, :] = jnp.zeros((8, cols), jnp.int32)
    landx[16:144, :] = land[...]

    @pl.when(tile == 0)
    def _():
        for f in range(3):
            ext[f, 8:16, :] = jnp.zeros((8, cols), f32)
        landx[8:16, :] = jnp.zeros((8, cols), jnp.int32)

    @pl.when(tile == tiles - 1)
    def _():
        for f in range(3):
            ext[f, 144:152, :] = jnp.zeros((8, cols), f32)
        landx[144:152, :] = jnp.zeros((8, cols), jnp.int32)

    lane = lax.broadcasted_iota(jnp.int32, (8, cols), 1)
    rows_all = float(tiles * TS)
    wet_mid = wet_line(depth, level, tile, lane, across)
    wet_low = wet_line(depth, level, (tile + tiles - 1) % tiles, lane, across)
    wet_high = wet_line(depth, level, (tile + 1) % tiles, lane, across)

    def rows_of(k, wet, store):
        feature_rows(
            k, tile, rows_all, wet, ext, landx, east, north, tracer, feat, act, act0, store
        )

    def inner(k, carry):
        rows_of(k, wet_mid, True)
        return carry

    lax.fori_loop(1, 15, inner, 0)

    @pl.when(tile > 0)
    def _():
        for f in range(4):
            halo_copy(0, f).wait_recv()

    @pl.when(tile < tiles - 1)
    def _():
        for f in range(4):
            halo_copy(1, f).wait_recv()

    rows_of(-1, wet_low, False)
    rows_of(0, wet_mid, True)
    rows_of(15, wet_mid, True)
    rows_of(16, wet_high, False)

    def window_copy(slot, part):
        group, place = ((2, 0), (3, 0), (3, 1))[slot]
        src, dst = ((main_out, main_in), (edge_out, edge_in))[part]
        return pltpu.make_async_remote_copy(
            src_ref=src.at[slot],
            dst_ref=dst.at[place],
            send_sem=win_send.at[slot, part],
            recv_sem=win_recv.at[place, part],
            device_id=(group, tile),
            device_id_type=mesh_id,
        )

    @pl.when(level == 0)
    def _():
        for slot in (1, 0, 2):
            lane0 = (KEPT + slot) * TS
            main_out[slot] = feat[:, :, lane0 : lane0 + TS].astype(bf16)
            edge = feat[:, :, lane0 + TS : lane0 + 2 * TS].reshape(432, TS).astype(bf16)
            edge_out[slot] = lax.dot_general(
                pick[...], edge, (((1,), (1,)), ((), ())), preferred_element_type=f32
            ).astype(bf16)
            for part in range(2):
                window_copy(slot, part).start()

    build_weights(w1, w2, w3, w1f, w1s, w2s, w3f, w3s)
    flat[...] = jnp.zeros_like(flat)
    feat_out[...] = feat[...].astype(bf16)
    act_out[...] = act[...]

    def result_copy(item):
        return pltpu.make_async_remote_copy(
            src_ref=res_out.at[item],
            dst_ref=res_in.at[level - 2 + item],
            send_sem=res_send.at[item],
            recv_sem=res_recv.at[level - 2 + item],
            device_id=(0, tile),
            device_id_type=mesh_id,
        )

    def item_step(item, carry):
        lane0 = pl.multiple_of(item * TS, TS)

        @pl.when(level == 0)
        def _():
            win[...] = feat[:, :, pl.ds(lane0, 2 * TS)]
            mwin[...] = act[:, pl.ds(lane0, 2 * TS)]

        @pl.when(level >= 2)
        def _():
            for part in range(2):
                src, dst = ((main_out, main_in), (edge_out, edge_in))[part]
                pltpu.make_async_remote_copy(
                    src_ref=src.at[0],
                    dst_ref=dst.at[item],
                    send_sem=win_send.at[0, part],
                    recv_sem=win_recv.at[item, part],
                    device_id=(0, tile),
                    device_id_type=mesh_id,
                ).wait_recv()
            win[:, :, 0:TS] = main_in[item].astype(f32)
            edge = lax.dot_general(
                edge_in[item], pick[...], (((0,), (0,)), ((), ())), preferred_element_type=f32
            )
            win[:, :, TS : 2 * TS] = edge.reshape(3, 144, TS)
            from0 = pl.multiple_of((KEPT + level - 2 + item) * TS, TS)
            mwin[...] = act0[:, pl.ds(from0, 2 * TS)]

        closure_tile(
            win, mwin, res, sel_in, sel_out, b1, b2, b3, w1s, w2s, w3s, patches, h1, h2, parts, flat
        )

        @pl.when(level == 0)
        def _():
            add_push(east, north, res, lane0)

        @pl.when(level >= 2)
        def _():
            res_out[item] = res[...]
            result_copy(item).start()

        return carry

    here = jnp.where(level == 0, KEPT, jnp.where(level == 1, 0, level - 1))
    lax.fori_loop(0, here, item_step, 0)

    @pl.when(level == 0)
    def _():
        for slot in range(3):
            pltpu.make_async_remote_copy(
                src_ref=res_out.at[0],
                dst_ref=res_in.at[slot],
                send_sem=res_send.at[0],
                recv_sem=res_recv.at[slot],
                device_id=(3, tile),
                device_id_type=mesh_id,
            ).wait_recv()
            lane0 = (KEPT + slot) * TS
            east[:, lane0 : lane0 + TS] += res_in[slot, 0]
            north[:, lane0 : lane0 + TS] += res_in[slot, 1]
            for part in range(2):
                window_copy(slot, part).wait_send()

    @pl.when(level == 2)
    def _():
        result_copy(0).wait_send()

    @pl.when(level == 3)
    def _():
        result_copy(0).wait_send()
        result_copy(1).wait_send()

    @pl.when(tile < tiles - 1)
    def _():
        for f in range(4):
            halo_copy(0, f).wait_send()

    @pl.when(tile > 0)
    def _():
        for f in range(4):
            halo_copy(1, f).wait_send()


def second_kernel(
    depth, meta, b3, east1, north1, feat, act, w1s, w2s, w3s, b1, b2, sel_in, sel_out,
    east, north,
    patches, h1, h2, parts, flat, win, mwin, res,
):
    level, tile = meta[0], meta[1]
    across = east.shape[1] // TS
    east[...] = east1[...]
    north[...] = north1[...]

    @pl.when(level > 0)
    def _():
        flat[...] = jnp.zeros_like(flat)

        def column(ty, carry):
            @pl.when(depth[tile * across + ty] > level)
            def _():
                lane0 = pl.multiple_of(ty * TS, TS)
                win[...] = feat[:, :, pl.ds(lane0, 2 * TS)].astype(f32)
                mwin[...] = act[:, pl.ds(lane0, 2 * TS)]
                closure_tile(
                    win, mwin, res, sel_in, sel_out, b1, b2, b3, w1s, w2s, w3s,
                    patches, h1, h2, parts, flat,
                )
                add_push(east, north, res, lane0)

            return carry

        lax.fori_loop(0, across, column, 0)


def body(u, v, t, land, depth, conv_one, bias_one, conv_two, bias_two, conv_three, bias_three):
    levels, rows, cols = u.shape
    w1 = conv_one.transpose(1, 3, 2, 0).astype(f32)
    w2 = conv_two.transpose(2, 3, 1, 0).astype(f32)
    w3 = conv_three.transpose(0, 2, 3, 1).astype(f32)
    b1 = jnp.tile(0.5 * bias_one, 4)[None]
    b2 = jnp.tile(0.5 * bias_two, 4)[None]
    sel_in = jnp.asarray(select_in(), bf16)
    sel_out = jnp.asarray(select_out(), bf16)
    pick = jnp.asarray(np.eye(16, TS, dtype=np.float32), bf16)
    meta = jnp.stack([lax.axis_index("group"), lax.axis_index("tile")]).astype(jnp.int32)
    vmem = pl.BlockSpec(memory_space=pltpu.VMEM)
    smem = pl.BlockSpec(memory_space=pltpu.SMEM)
    wide = cols + TS
    plane = jax.ShapeDtypeStruct((rows, cols), f32)
    work = [
        pltpu.VMEM((9, SLAB, TS), bf16),
        pltpu.VMEM((ROWS1 + 1, SLAB, 256), bf16),
        pltpu.VMEM((ROWS2, SLAB, 256), bf16),
        pltpu.VMEM((ROWS2, 64, SLAB), f32),
        pltpu.VMEM((2, 3, 72, SLAB), f32),
        pltpu.VMEM((3, 144, 2 * TS), f32),
        pltpu.VMEM((144, 2 * TS), f32),
        pltpu.VMEM((2, TS, TS), f32),
    ]
    east1, north1, tracer, feat, act, w1s, w2s, w3s = pl.pallas_call(
        first_kernel,
        out_shape=[plane] * 3
        + [
            jax.ShapeDtypeStruct((3, 144, wide), bf16),
            jax.ShapeDtypeStruct((144, wide), f32),
            jax.ShapeDtypeStruct((4, 256, 256), bf16),
            jax.ShapeDtypeStruct((4, 256, 256), bf16),
            jax.ShapeDtypeStruct((64, 256), bf16),
        ],
        in_specs=[smem] * 2 + [vmem] * 12,
        out_specs=[vmem] * 8,
        scratch_shapes=[
            pltpu.VMEM((3, 160, cols), f32),
            pltpu.VMEM((160, cols), jnp.int32),
            pltpu.VMEM((3, 144, wide), f32),
            pltpu.VMEM((144, wide), f32),
            pltpu.VMEM((144, wide), f32),
            pltpu.VMEM((4, 256, 256), f32),
            pltpu.VMEM((64, 256), f32),
        ]
        + work
        + [
            pltpu.VMEM((3, 3, 144, TS), bf16),
            pltpu.VMEM((3, 16, 432), bf16),
            pltpu.VMEM((2, 3, 144, TS), bf16),
            pltpu.VMEM((2, 16, 432), bf16),
            pltpu.VMEM((2, 2, TS, TS), f32),
            pltpu.VMEM((3, 2, TS, TS), f32),
            pltpu.SemaphoreType.DMA((2, 4)),
            pltpu.SemaphoreType.DMA((2, 4)),
            pltpu.SemaphoreType.DMA((3, 2)),
            pltpu.SemaphoreType.DMA((2, 2)),
            pltpu.SemaphoreType.DMA((2,)),
            pltpu.SemaphoreType.DMA((3,)),
        ],
        compiler_params=pltpu.CompilerParams(
            vmem_limit_bytes=40 * 2**20, collective_id=0, has_side_effects=True
        ),
        name="first",
    )(depth, bias_three, u[0], v[0], t[0], land, w1, b1, w2, b2, w3, sel_in, sel_out, pick)
    east, north = pl.pallas_call(
        second_kernel,
        out_shape=[plane] * 2,
        in_specs=[smem] * 3 + [vmem] * 11,
        out_specs=[vmem] * 2,
        scratch_shapes=work,
        compiler_params=pltpu.CompilerParams(vmem_limit_bytes=40 * 2**20),
        name="second",
    )(depth, meta, bias_three, east1, north1, feat, act, w1s, w2s, w3s, b1, b2, sel_in, sel_out)
    return east[None], north[None], tracer[None]


def solution(mesh):
    field = P("group", "tile", None)
    in_specs = (field, field, field, P("tile", None)) + (P(),) * 7
    return jax.shard_map(
        body, mesh=mesh, in_specs=in_specs, out_specs=(field,) * 3, check_vma=False
    )
```

```python
import jax
import jax.numpy as jnp
from jax import lax
from jax.experimental import pallas as pl
from jax.experimental.pallas import tpu as pltpu
from jax.sharding import PartitionSpec as P

time_step = 0.1
viscosity = 0.5
diffusivity = 0.5
eddy_gain = 0.5
coriolis_base = 0.2
coriolis_slope = 0.6

bf16 = jnp.bfloat16
f32 = jnp.float32

TS = 128
HALO = 5
ROWS1, ROWS2, ROWS3 = 35, 34, 33
SLAB = 160
USED = 144


def build_tables(sel_in, sel_out, pick):
    row = lax.broadcasted_iota(jnp.int32, (80, 256), 0)
    col = lax.broadcasted_iota(jnp.int32, (80, 256), 1)
    sel_in[...] = (col == 2 * (9 * (row % 8) + row // 8)).astype(f32).astype(bf16)
    row = lax.broadcasted_iota(jnp.int32, (160, 256), 0)
    col = lax.broadcasted_iota(jnp.int32, (160, 256), 1)
    place = 2 * (9 * (row % 8) + row // 16)
    inside = (row < USED) & (col < 130)
    for ip in range(2):
        for b in range(2):
            hit = inside & ((row % 16) // 8 == ip) & (col == place + b)
            sel_out[ip, b] = hit.astype(f32).astype(bf16)
    row = lax.broadcasted_iota(jnp.int32, (16, TS), 0)
    col = lax.broadcasted_iota(jnp.int32, (16, TS), 1)
    pick[...] = (row == col).astype(f32).astype(bf16)


def taps():
    for outer in range(2):
        for inner in range(2):
            for out in range(2):
                k = 2 * outer + inner - out
                if 0 <= k < 3:
                    yield outer, inner, out, k


def build_weights(w1, w2, w3, b1, b2, w1f, w1s, w2s, w3f, w3s, b1r, b2r):
    w1f[...] = jnp.zeros_like(w1f)
    for c in range(3):
        for kx in range(3):
            line = 0.5 * w1[c, kx].astype(f32)
            for q in range(4):
                for dj, dy, b, ky in taps():
                    for a in range(2):
                        row = dj * 128 + dy * 48 + c * 16 + 4 + 2 * q + a + kx
                        lane = (a * 2 + b) * 64
                        w1f[q, row : row + 1, lane : lane + 64] = line[ky : ky + 1]
    w1s[...] = w1f[...].astype(bf16)
    w2s[...] = jnp.zeros_like(w2s)
    for kx in range(3):
        for ky in range(3):
            block = (0.5 * w2[kx, ky].astype(f32)).T.astype(bf16)
            for di, ai, ao, kx_here in taps():
                for dj, bi, bo, ky_here in taps():
                    if (kx, ky) == (kx_here, ky_here):
                        row = (ai * 2 + bi) * 64
                        lane = (ao * 2 + bo) * 64
                        w2s[di * 2 + dj, row : row + 64, lane : lane + 64] = block
    w3f[...] = jnp.zeros_like(w3f)
    for c in range(3):
        for kx in range(3):
            line = w3[c, kx].astype(f32)
            for di, ai, ao, kx_here in taps():
                if kx != kx_here:
                    continue
                for dj, bi, bo, ky in taps():
                    lane = (ai * 2 + bi) * 64
                    row = (di * 2 + dj) * 16 + bo * 6 + c * 2 + ao
                    w3f[row : row + 1, lane : lane + 64] = line[ky : ky + 1]
    w3s[...] = w3f[...].astype(bf16)
    for j in range(4):
        b1r[:, 64 * j : 64 * j + 64] = 0.5 * b1[...]
        b2r[:, 64 * j : 64 * j + 64] = 0.5 * b2[...]


def wet_line(depth, level, tile_row, lane, across):
    line = jnp.zeros(lane.shape, f32)
    for ty in range(across):
        wet = (depth[tile_row * across + ty] > level).astype(f32)
        line = jnp.where(lane // TS == ty, wet, line)
    return line


def feature_rows(k, tile, rows_all, wet, ext, landx, east, north, tracer, feat, act, act0, store):
    cols = landx.shape[1]
    lane = lax.broadcasted_iota(jnp.int32, (8, cols), 1)
    row = lax.broadcasted_iota(jnp.int32, (8, cols), 0)
    zeros = jnp.zeros((8, TS), f32)

    def west(x):
        return jnp.where(lane == 0, 0.0, pltpu.roll(x, 1, 1))

    def east_of(x):
        return jnp.where(lane == cols - 1, 0.0, pltpu.roll(x, cols - 1, 1))

    base = 8 * k + 16
    if not isinstance(k, int):
        base = pl.multiple_of(base, 8)
    water = jnp.where(landx[pl.ds(base, 8), :] == 1, 1.0, 0.0)
    active = water * wet
    above = base - 8 if isinstance(k, int) else pl.multiple_of(base - 8, 8)
    around = [ext[f, pl.ds(above, 24), :] for f in range(3)]
    mid = [x[8:16] for x in around]
    up = [x[7:15] for x in around]
    down = [x[9:17] for x in around]
    left = [west(x) for x in mid]
    right = [east_of(x) for x in mid]
    lap = [down[f] + up[f] + right[f] + left[f] - 4.0 * mid[f] for f in range(3)]
    grad_east = 0.5 * (down[2] - up[2])
    grad_north = 0.5 * (right[2] - left[2])
    place = (tile * TS + 8 * k + row).astype(f32)
    coriolis = coriolis_base + coriolis_slope * (place + 0.5) / rows_all
    step = time_step * active
    new_east = mid[0] + step * (coriolis * mid[1] - grad_east + viscosity * lap[0])
    new_north = mid[1] + step * (-coriolis * mid[0] - grad_north + viscosity * lap[1])
    new_tracer = mid[2] + step * (
        -(mid[0] * grad_east + mid[1] * grad_north) + diffusivity * lap[2]
    )
    if store:
        at = 8 * k
        if not isinstance(k, int):
            at = pl.multiple_of(at, 8)
        east[pl.ds(at, 8), :] = new_east
        north[pl.ds(at, 8), :] = new_north
        tracer[pl.ds(at, 8), :] = new_tracer
    q = 8 * k + 8
    if not isinstance(k, int):
        q = pl.multiple_of(q, 8)
    for c, new in enumerate((new_east, new_north, new_tracer)):
        wide = jnp.concatenate([new * active, zeros], axis=1)
        feat[c, pl.ds(q, 8), :] = pltpu.roll(wide, 4, 1)
    act[pl.ds(q, 8), :] = pltpu.roll(jnp.concatenate([active, zeros], axis=1), 1, 1)
    act0[pl.ds(q, 8), :] = pltpu.roll(jnp.concatenate([water, zeros], axis=1), 1, 1)


def silu_half(half):
    return half + half * jnp.tanh(half)


def store_slab(ref, index, value):
    ref[index, 0:USED, :] = value.astype(bf16)
    ref[index, USED:SLAB, :] = pltpu.roll(value[0:16], 15, 0).astype(bf16)


def closure_tile(win, mwin, res, sel_in, sel_out, b1, b2, b3, w1s, w2s, w3s, patches, h1, h2, parts, flat):
    for g in range(9):
        halves = []
        for ip in range(2):
            base = 64 * ip + 8 * g
            rows = win[:, base : base + 16, :].reshape(48, 256)
            rows = jnp.concatenate([rows, pltpu.roll(rows, 255, 1), jnp.zeros((32, 256), f32)], axis=0)
            got = lax.dot_general(
                sel_in[...], rows.astype(bf16), (((1,), (1,)), ((), ())), preferred_element_type=f32
            )
            halves.append(got.reshape(10, 8, 128))
        patches[g] = jnp.stack(halves, axis=1).reshape(SLAB, 128).astype(bf16)
    for q in range(4):
        for g in range(9):
            if 4 * g + q >= ROWS1:
                continue
            lhs = jnp.concatenate([patches[g, 0:USED, :], patches[g, 16:SLAB, :]], axis=1)
            half = jnp.dot(lhs, w1s[q], preferred_element_type=f32) + b1[...]
            store_slab(h1, 4 * g + q, silu_half(half))
    for i in range(0, ROWS2, 2):
        half = b2[...]
        for di in range(2):
            for dj in range(2):
                lhs = h1[i + di : i + di + 2, 16 * dj : 16 * dj + USED, :].reshape(2 * USED, 256)
                half = half + jnp.dot(lhs, w2s[2 * di + dj], preferred_element_type=f32)
        out = silu_half(half)
        store_slab(h2, i, out[0:USED])
        store_slab(h2, i + 1, out[USED:])
    for i in range(ROWS2):
        parts[i] = lax.dot_general(
            w3s[...], h2[i], (((1,), (1,)), ((), ())), preferred_element_type=f32
        )
    for i in range(ROWS3):
        got = (
            parts[i, 0:16, 0:USED]
            + parts[i, 16:32, 16:SLAB]
            + parts[i + 1, 32:48, 0:USED]
            + parts[i + 1, 48:64, 16:SLAB]
        )
        for b in range(2):
            for c in range(3):
                r = b * 6 + c * 2
                flat[b, c, 2 * i : 2 * i + 2, 0:USED] = got[r : r + 2] + b3[c]
    for ip in range(2):
        mask = mwin[8 + 64 * ip - 1 : 8 + 64 * ip + 65, :]
        masked = []
        for c in range(3):
            image = jnp.zeros((72, 256), f32)
            for b in range(2):
                image = image + jnp.dot(
                    flat[b, c].astype(bf16), sel_out[ip, b], preferred_element_type=f32
                )
            masked.append(image[0:66] * mask)
        xx, xy, yy = masked

        def dx(m):
            return 0.5 * (m[2:66, 1:129] - m[0:64, 1:129])

        def dy(m):
            return 0.5 * (m[1:65, 2:130] - m[1:65, 0:128])

        gain = eddy_gain * mask[1:65, 1:129]
        rows = slice(64 * ip, 64 * ip + 64)
        res[0, rows, :] = gain * (dx(xx) + dy(xy))
        res[1, rows, :] = gain * (dx(xy) + dy(yy))


def add_push(east, north, res, lane0):
    east[:, pl.ds(lane0, TS)] += res[0]
    north[:, pl.ds(lane0, TS)] += res[1]


KEPT = 5


def first_kernel(
    depth, b3, u, v, t, land, w1h, w2h, w3h, b1h, b2h,
    east, north, tracer, feat_out, act_out, w1s, w2s, w3s, b1r, b2r, sel_in, sel_out,
    ext, landx, feat, act, act0, w1f, w3f, w1, w2, w3, b1, b2, pick,
    patches, h1, h2, parts, flat, win, mwin, res,
    main_out, edge_out, main_in, edge_in, res_out, res_in,
    load_sem, halo_send, halo_recv, win_send, win_recv, res_send, res_recv,
):
    level, tile = lax.axis_index("group"), lax.axis_index("tile")
    tiles = lax.axis_size("tile")
    cols = u.shape[1]
    across = cols // TS
    mesh_id = pl.DeviceIdType.MESH

    loads = [
        pltpu.make_async_copy(origin, place, load_sem.at[i])
        for i, (origin, place) in enumerate(
            (
                (u, ext.at[0, pl.ds(16, TS)]),
                (v, ext.at[1, pl.ds(16, TS)]),
                (t, ext.at[2, pl.ds(16, TS)]),
                (land, landx.at[pl.ds(16, TS)]),
                (w1h, w1),
                (w2h, w2),
                (w3h, w3),
                (b1h, b1),
                (b2h, b2),
            )
        )
    ]
    for load in loads:
        load.start()

    barrier = pltpu.get_barrier_semaphore()

    def greet(group, place):
        pl.semaphore_signal(barrier, inc=1, device_id=(group, place), device_id_type=mesh_id)

    @pl.when(tile > 0)
    def _():
        greet(level, tile - 1)

    @pl.when(tile < tiles - 1)
    def _():
        greet(level, tile + 1)

    @pl.when(level == 0)
    def _():
        greet(2, tile)
        greet(3, tile)

    @pl.when(level >= 2)
    def _():
        greet(0, tile)

    peers = jnp.where(tile > 0, 1, 0) + jnp.where(tile < tiles - 1, 1, 0)
    peers = peers + jnp.where(level == 0, 2, jnp.where(level == 1, 0, 1))

    for f in range(3):
        ext[f, 0:8, :] = jnp.zeros((8, cols), f32)
        ext[f, 152:160, :] = jnp.zeros((8, cols), f32)
    landx[0:8, :] = jnp.zeros((8, cols), jnp.int32)
    landx[152:160, :] = jnp.zeros((8, cols), jnp.int32)
    build_tables(sel_in, sel_out, pick)
    pl.semaphore_wait(barrier, peers)

    def halo_copy(way, f):
        src = (u, v, t, land)[f]
        rows_from, rows_to, place = ((TS - 8, 8, tile + 1), (0, 144, tile - 1))[way]
        dst = ext.at[f, pl.ds(rows_to, 8)] if f < 3 else landx.at[pl.ds(rows_to, 8)]
        return pltpu.make_async_remote_copy(
            src_ref=src.at[pl.ds(rows_from, 8)],
            dst_ref=dst,
            send_sem=halo_send.at[way, f],
            recv_sem=halo_recv.at[way, f],
            device_id=(level, place),
            device_id_type=mesh_id,
        )

    @pl.when(tile < tiles - 1)
    def _():
        for f in range(4):
            halo_copy(0, f).start()

    @pl.when(tile > 0)
    def _():
        for f in range(4):
            halo_copy(1, f).start()

    @pl.when(tile == 0)
    def _():
        for f in range(3):
            ext[f, 8:16, :] = jnp.zeros((8, cols), f32)
        landx[8:16, :] = jnp.zeros((8, cols), jnp.int32)

    @pl.when(tile == tiles - 1)
    def _():
        for f in range(3):
            ext[f, 144:152, :] = jnp.zeros((8, cols), f32)
        landx[144:152, :] = jnp.zeros((8, cols), jnp.int32)

    lane = lax.broadcasted_iota(jnp.int32, (8, cols), 1)
    rows_all = float(tiles * TS)
    wet_mid = wet_line(depth, level, tile, lane, across)
    wet_low = wet_line(depth, level, (tile + tiles - 1) % tiles, lane, across)
    wet_high = wet_line(depth, level, (tile + 1) % tiles, lane, across)

    def rows_of(k, wet, store):
        feature_rows(
            k, tile, rows_all, wet, ext, landx, east, north, tracer, feat, act, act0, store
        )

    def inner(k, carry):
        rows_of(k, wet_mid, True)
        return carry

    for load in loads[:4]:
        load.wait()
    lax.fori_loop(1, 15, inner, 0)

    def window_copy(slot, part):
        group, place = ((2, 0), (3, 0), (3, 1))[slot]
        if part == 3:
            src, dst = edge_out.at[slot], edge_in.at[place]
        else:
            rows = pl.ds(*((16, 112), (0, 16), (128, 16))[part])
            src, dst = main_out.at[slot, :, rows], main_in.at[place, :, rows]
        return pltpu.make_async_remote_copy(
            src_ref=src,
            dst_ref=dst,
            send_sem=win_send.at[slot, part],
            recv_sem=win_recv.at[place, part],
            device_id=(group, tile),
            device_id_type=mesh_id,
        )

    @pl.when(level == 0)
    def _():
        for slot in (1, 0, 2):
            lane0 = (KEPT + slot) * TS
            main_out[slot, :, 16:128] = feat[:, 16:128, lane0 : lane0 + TS].astype(bf16)
            window_copy(slot, 0).start()

    for load in loads[4:]:
        load.wait()
    build_weights(w1, w2, w3, b1, b2, w1f, w1s, w2s, w3f, w3s, b1r, b2r)
    flat[...] = jnp.zeros_like(flat)

    @pl.when(tile > 0)
    def _():
        for f in range(4):
            halo_copy(0, f).wait_recv()

    @pl.when(tile < tiles - 1)
    def _():
        for f in range(4):
            halo_copy(1, f).wait_recv()

    rows_of(-1, wet_low, False)
    rows_of(0, wet_mid, True)
    rows_of(15, wet_mid, True)
    rows_of(16, wet_high, False)

    @pl.when(level == 0)
    def _():
        for slot in (1, 0, 2):
            lane0 = (KEPT + slot) * TS
            for part, rows in ((1, slice(0, 16)), (2, slice(128, 144))):
                main_out[slot, :, rows] = feat[:, rows, lane0 : lane0 + TS].astype(bf16)
                window_copy(slot, part).start()
            edge = feat[:, :, lane0 + TS : lane0 + 2 * TS].reshape(432, TS).astype(bf16)
            edge_out[slot] = lax.dot_general(
                pick[...], edge, (((1,), (1,)), ((), ())), preferred_element_type=f32
            ).astype(bf16)
            window_copy(slot, 3).start()

    feat_out[...] = feat[...].astype(bf16)
    act_out[...] = act[...]

    def result_copy(item):
        return pltpu.make_async_remote_copy(
            src_ref=res_out.at[item],
            dst_ref=res_in.at[level - 2 + item],
            send_sem=res_send.at[item],
            recv_sem=res_recv.at[level - 2 + item],
            device_id=(0, tile),
            device_id_type=mesh_id,
        )

    def item_step(item, carry):
        lane0 = pl.multiple_of(item * TS, TS)

        @pl.when(level == 0)
        def _():
            win[...] = feat[:, :, pl.ds(lane0, 2 * TS)]
            mwin[...] = act[:, pl.ds(lane0, 2 * TS)]

        @pl.when(level >= 2)
        def _():
            for part in range(4):
                if part == 3:
                    src, dst = edge_out.at[0], edge_in.at[item]
                else:
                    rows = pl.ds(*((16, 112), (0, 16), (128, 16))[part])
                    src, dst = main_out.at[0, :, rows], main_in.at[item, :, rows]
                pltpu.make_async_remote_copy(
                    src_ref=src,
                    dst_ref=dst,
                    send_sem=win_send.at[0, part],
                    recv_sem=win_recv.at[item, part],
                    device_id=(0, tile),
                    device_id_type=mesh_id,
                ).wait_recv()
            win[:, :, 0:TS] = main_in[item].astype(f32)
            edge = lax.dot_general(
                edge_in[item], pick[...], (((0,), (0,)), ((), ())), preferred_element_type=f32
            )
            win[:, :, TS : 2 * TS] = edge.reshape(3, 144, TS)
            from0 = pl.multiple_of((KEPT + level - 2 + item) * TS, TS)
            mwin[...] = act0[:, pl.ds(from0, 2 * TS)]

        closure_tile(
            win, mwin, res, sel_in, sel_out, b1r, b2r, b3, w1s, w2s, w3s, patches, h1, h2, parts, flat
        )

        @pl.when(level == 0)
        def _():
            add_push(east, north, res, lane0)

        @pl.when(level >= 2)
        def _():
            res_out[item] = res[...]
            result_copy(item).start()

        return carry

    here = jnp.where(level == 0, KEPT, jnp.where(level == 1, 0, level - 1))
    lax.fori_loop(0, here, item_step, 0)

    @pl.when(level == 0)
    def _():
        for slot in range(3):
            pltpu.make_async_remote_copy(
                src_ref=res_out.at[0],
                dst_ref=res_in.at[slot],
                send_sem=res_send.at[0],
                recv_sem=res_recv.at[slot],
                device_id=(3, tile),
                device_id_type=mesh_id,
            ).wait_recv()
            lane0 = (KEPT + slot) * TS
            east[:, lane0 : lane0 + TS] += res_in[slot, 0]
            north[:, lane0 : lane0 + TS] += res_in[slot, 1]
            for part in range(4):
                window_copy(slot, part).wait_send()

    @pl.when(level == 2)
    def _():
        result_copy(0).wait_send()

    @pl.when(level == 3)
    def _():
        result_copy(0).wait_send()
        result_copy(1).wait_send()

    @pl.when(tile < tiles - 1)
    def _():
        for f in range(4):
            halo_copy(0, f).wait_send()

    @pl.when(tile > 0)
    def _():
        for f in range(4):
            halo_copy(1, f).wait_send()


def second_kernel(
    depth, b3, east1, north1, tracer1, feat, act, w1s, w2s, w3s, b1, b2, sel_in, sel_out,
    east, north, tracer,
    sums, patches, h1, h2, parts, flat, win, mwin, res,
    tracer_sem, out_sem,
):
    level, tile = lax.axis_index("group"), lax.axis_index("tile")
    across = east1.shape[1] // TS
    tracer_copy = pltpu.make_async_copy(tracer1, tracer, tracer_sem)
    tracer_copy.start()
    sums[0] = east1[...]
    sums[1] = north1[...]
    flat[...] = jnp.zeros_like(flat)

    def block_copy(ty, which):
        lanes = pl.ds(pl.multiple_of(ty * TS, TS), TS)
        return pltpu.make_async_copy(
            sums.at[which, :, lanes], (east, north)[which].at[:, lanes], out_sem.at[ty, which]
        )

    def column(ty, carry):
        @pl.when((level > 0) & (depth[tile * across + ty] > level))
        def _():
            lane0 = pl.multiple_of(ty * TS, TS)
            win[...] = feat[:, :, pl.ds(lane0, 2 * TS)].astype(f32)
            mwin[...] = act[:, pl.ds(lane0, 2 * TS)]
            closure_tile(
                win, mwin, res, sel_in, sel_out, b1, b2, b3, w1s, w2s, w3s,
                patches, h1, h2, parts, flat,
            )
            for which in range(2):
                sums[which, :, pl.ds(lane0, TS)] += res[which]

        for which in range(2):
            block_copy(ty, which).start()
        return carry

    lax.fori_loop(0, across, column, 0)

    def drain(ty, carry):
        for which in range(2):
            block_copy(ty, which).wait()
        return carry

    lax.fori_loop(0, across, drain, 0)
    tracer_copy.wait()


def body(u, v, t, land, depth, conv_one, bias_one, conv_two, bias_two, conv_three, bias_three):
    levels, rows, cols = u.shape
    vmem = pl.BlockSpec(memory_space=pltpu.VMEM)
    smem = pl.BlockSpec(memory_space=pltpu.SMEM)
    hbm = pl.BlockSpec(memory_space=pltpu.HBM)
    wide = cols + TS
    across = cols // TS
    plane = jax.ShapeDtypeStruct((rows, cols), f32)
    work = [
        pltpu.VMEM((9, SLAB, TS), bf16),
        pltpu.VMEM((ROWS1 + 1, SLAB, 256), bf16),
        pltpu.VMEM((ROWS2, SLAB, 256), bf16),
        pltpu.VMEM((ROWS2, 64, SLAB), f32),
        pltpu.VMEM((2, 3, 72, SLAB), f32),
        pltpu.VMEM((3, 144, 2 * TS), f32),
        pltpu.VMEM((144, 2 * TS), f32),
        pltpu.VMEM((2, TS, TS), f32),
    ]
    def stay(x):
        return pltpu.with_memory_space_constraint(x, pltpu.HBM)

    east1, north1, tracer1, feat, act, w1s, w2s, w3s, b1r, b2r, sel_in, sel_out = pl.pallas_call(
        first_kernel,
        out_shape=[plane] * 3
        + [
            jax.ShapeDtypeStruct((3, 144, wide), bf16),
            jax.ShapeDtypeStruct((144, wide), f32),
            jax.ShapeDtypeStruct((4, 256, 256), bf16),
            jax.ShapeDtypeStruct((4, 256, 256), bf16),
            jax.ShapeDtypeStruct((64, 256), bf16),
            jax.ShapeDtypeStruct((1, 256), f32),
            jax.ShapeDtypeStruct((1, 256), f32),
            jax.ShapeDtypeStruct((80, 256), bf16),
            jax.ShapeDtypeStruct((2, 2, SLAB, 256), bf16),
        ],
        in_specs=[smem] * 2 + [hbm] * 9,
        out_specs=[vmem] * 12,
        scratch_shapes=[
            pltpu.VMEM((3, 160, cols), f32),
            pltpu.VMEM((160, cols), jnp.int32),
            pltpu.VMEM((3, 144, wide), f32),
            pltpu.VMEM((144, wide), f32),
            pltpu.VMEM((144, wide), f32),
            pltpu.VMEM((4, 256, 256), f32),
            pltpu.VMEM((64, 256), f32),
            pltpu.VMEM((3, 3, 3, 64), bf16),
            pltpu.VMEM((3, 3, 64, 64), bf16),
            pltpu.VMEM((3, 3, 3, 64), bf16),
            pltpu.VMEM((1, 64), f32),
            pltpu.VMEM((1, 64), f32),
            pltpu.VMEM((16, TS), bf16),
        ]
        + work
        + [
            pltpu.VMEM((3, 3, 144, TS), bf16),
            pltpu.VMEM((3, 16, 432), bf16),
            pltpu.VMEM((2, 3, 144, TS), bf16),
            pltpu.VMEM((2, 16, 432), bf16),
            pltpu.VMEM((2, 2, TS, TS), f32),
            pltpu.VMEM((3, 2, TS, TS), f32),
            pltpu.SemaphoreType.DMA((9,)),
            pltpu.SemaphoreType.DMA((2, 4)),
            pltpu.SemaphoreType.DMA((2, 4)),
            pltpu.SemaphoreType.DMA((3, 4)),
            pltpu.SemaphoreType.DMA((2, 4)),
            pltpu.SemaphoreType.DMA((2,)),
            pltpu.SemaphoreType.DMA((3,)),
        ],
        compiler_params=pltpu.CompilerParams(
            vmem_limit_bytes=40 * 2**20, collective_id=0, has_side_effects=True
        ),
        name="first",
    )(
        depth, bias_three, stay(u[0]), stay(v[0]), stay(t[0]), stay(land),
        stay(conv_one.transpose(1, 2, 3, 0)), stay(conv_two.transpose(2, 3, 0, 1)),
        stay(conv_three.transpose(0, 2, 3, 1)), stay(bias_one[None]), stay(bias_two[None]),
    )
    east, north, tracer = pl.pallas_call(
        second_kernel,
        out_shape=[plane] * 3,
        in_specs=[smem] * 2 + [vmem] * 12,
        out_specs=[hbm] * 3,
        scratch_shapes=[pltpu.VMEM((2, rows, cols), f32)]
        + work
        + [pltpu.SemaphoreType.DMA, pltpu.SemaphoreType.DMA((across, 2))],
        compiler_params=pltpu.CompilerParams(vmem_limit_bytes=40 * 2**20),
        name="second",
    )(
        depth, bias_three, east1, north1, tracer1, feat, act, w1s, w2s, w3s, b1r, b2r,
        sel_in, sel_out,
    )
    return east[None], north[None], tracer[None]


def solution(mesh):
    field = P("group", "tile", None)
    in_specs = (field, field, field, P("tile", None)) + (P(),) * 7
    return jax.shard_map(
        body, mesh=mesh, in_specs=in_specs, out_specs=(field,) * 3, check_vma=False
    )
```

```python
import functools

import jax
import jax.numpy as jnp
from jax import lax
from jax.experimental import pallas as pl
from jax.experimental.pallas import tpu as pltpu
from jax.sharding import PartitionSpec as P

time_step = 0.1
viscosity = 0.5
diffusivity = 0.5
eddy_gain = 0.5
coriolis_base = 0.2
coriolis_slope = 0.6

bf16 = jnp.bfloat16
f32 = jnp.float32

TS = 128
HALO = 5
ROWS1, ROWS2 = 35, 34
SLAB = 160
USED = 144


def build_tables(sel_in, sel_out, pick):
    row = lax.broadcasted_iota(jnp.int32, (80, 256), 0)
    col = lax.broadcasted_iota(jnp.int32, (80, 256), 1)
    sel_in[...] = (col == 2 * (9 * (row % 8) + row // 8)).astype(f32).astype(bf16)
    row = lax.broadcasted_iota(jnp.int32, (USED, 256), 0)
    col = lax.broadcasted_iota(jnp.int32, (USED, 256), 1)
    place = 2 * (9 * (row % 8) + row // 16)
    inside = place + 1 < 130
    for ip in range(2):
        for b in range(2):
            hit = inside & ((row % 16) // 8 == ip) & (col == (place + b + 255) % 256)
            sel_out[ip, b] = hit.astype(f32).astype(bf16)
    row = lax.broadcasted_iota(jnp.int32, (16, TS), 0)
    col = lax.broadcasted_iota(jnp.int32, (16, TS), 1)
    pick[...] = (row == col).astype(f32).astype(bf16)


def taps():
    for outer in range(2):
        for inner in range(2):
            for out in range(2):
                k = 2 * outer + inner - out
                if 0 <= k < 3:
                    yield outer, inner, out, k


def build_weights(w1, w2, w3, b1, b2, w1f, w1s, w2s, w3f, w3s, b1r, b2r):
    w1f[...] = jnp.zeros_like(w1f)
    for c in range(3):
        for kx in range(3):
            line = 0.5 * w1[c, kx].astype(f32)
            for q in range(4):
                for dj, dy, b, ky in taps():
                    for a in range(2):
                        row = dj * 128 + dy * 48 + c * 16 + 4 + 2 * q + a + kx
                        lane = (a * 2 + b) * 64
                        w1f[q, row : row + 1, lane : lane + 64] = line[ky : ky + 1]
    w1s[...] = w1f[...].astype(bf16)
    w2s[...] = jnp.zeros_like(w2s)
    for kx in range(3):
        for ky in range(3):
            block = (0.5 * w2[kx, ky].astype(f32)).T.astype(bf16)
            for di, ai, ao, kx_here in taps():
                for dj, bi, bo, ky_here in taps():
                    if (kx, ky) == (kx_here, ky_here):
                        row = (ai * 2 + bi) * 64
                        lane = (ao * 2 + bo) * 64
                        w2s[di * 2 + dj, row : row + 64, lane : lane + 64] = block
    w3f[...] = jnp.zeros_like(w3f)
    for c in range(3):
        for kx in range(3):
            line = w3[c, kx].astype(f32)
            for di, ai, ao, kx_here in taps():
                if kx != kx_here:
                    continue
                for dj, bi, bo, ky in taps():
                    lane = (ai * 2 + bi) * 64
                    row = (di * 2 + dj) * 16 + bo * 6 + c * 2 + ao
                    w3f[row : row + 1, lane : lane + 64] = line[ky : ky + 1]
    turned = w3f[...].T.astype(bf16)
    row = lax.broadcasted_iota(jnp.int32, (64, 256), 0)
    col = lax.broadcasted_iota(jnp.int32, (64, 256), 1)
    part = row % 16
    di, dj = row // 32, (row // 16) % 2
    b, c, a = part // 6, (part % 6) // 2, part % 2
    for j in range(8):
        into = jnp.where(j - di >= 0, c * 16 + 2 * (j - di), 48 + 2 * c)
        hit = (part < 12) & (col == dj * 128 + b * 64 + into + a)
        spread = jnp.dot(turned, hit.astype(f32).astype(bf16), preferred_element_type=f32)
        w3s[256 * j : 256 * j + 256, :] = spread.astype(bf16)
    for j in range(4):
        b1r[:, 64 * j : 64 * j + 64] = 0.5 * b1[...]
        b2r[:, 64 * j : 64 * j + 64] = 0.5 * b2[...]


def wet_line(depth, level, tile_row, lane, across):
    line = jnp.zeros(lane.shape, f32)
    for ty in range(across):
        wet = (depth[tile_row * across + ty] > level).astype(f32)
        line = jnp.where(lane // TS == ty, wet, line)
    return line


def feature_rows(k, tile, rows_all, wet, ext, landx, east, north, tracer, feat, act, act0, store):
    cols = landx.shape[1]
    lane = lax.broadcasted_iota(jnp.int32, (8, cols), 1)
    row = lax.broadcasted_iota(jnp.int32, (8, cols), 0)
    zeros = jnp.zeros((8, TS), f32)

    def west(x):
        return jnp.where(lane == 0, 0.0, pltpu.roll(x, 1, 1))

    def east_of(x):
        return jnp.where(lane == cols - 1, 0.0, pltpu.roll(x, cols - 1, 1))

    base = 8 * k + 16
    if not isinstance(k, int):
        base = pl.multiple_of(base, 8)
    water = jnp.where(landx[pl.ds(base, 8), :] == 1, 1.0, 0.0)
    active = water * wet
    above = base - 8 if isinstance(k, int) else pl.multiple_of(base - 8, 8)
    around = [ext[f, pl.ds(above, 24), :] for f in range(3)]
    mid = [x[8:16] for x in around]
    up = [x[7:15] for x in around]
    down = [x[9:17] for x in around]
    left = [west(x) for x in mid]
    right = [east_of(x) for x in mid]
    lap = [down[f] + up[f] + right[f] + left[f] - 4.0 * mid[f] for f in range(3)]
    grad_east = 0.5 * (down[2] - up[2])
    grad_north = 0.5 * (right[2] - left[2])
    place = (tile * TS + 8 * k + row).astype(f32)
    coriolis = coriolis_base + coriolis_slope * (place + 0.5) / rows_all
    step = time_step * active
    new_east = mid[0] + step * (coriolis * mid[1] - grad_east + viscosity * lap[0])
    new_north = mid[1] + step * (-coriolis * mid[0] - grad_north + viscosity * lap[1])
    new_tracer = mid[2] + step * (
        -(mid[0] * grad_east + mid[1] * grad_north) + diffusivity * lap[2]
    )
    if store:
        at = 8 * k
        if not isinstance(k, int):
            at = pl.multiple_of(at, 8)
        east[pl.ds(at, 8), :] = new_east
        north[pl.ds(at, 8), :] = new_north
        tracer[pl.ds(at, 8), :] = new_tracer
    q = 8 * k + 8
    if not isinstance(k, int):
        q = pl.multiple_of(q, 8)
    for c, new in enumerate((new_east, new_north, new_tracer)):
        wide = jnp.concatenate([new * active, zeros], axis=1)
        feat[c, pl.ds(q, 8), :] = pltpu.roll(wide, 4, 1)
    act[pl.ds(q, 8), :] = pltpu.roll(jnp.concatenate([active, zeros], axis=1), 1, 1)
    act0[pl.ds(q, 8), :] = pltpu.roll(jnp.concatenate([water, zeros], axis=1), 1, 1)


def silu_half(half):
    return half + half * jnp.tanh(half)


def store_slab(ref, index, value):
    ref[index, 0:USED, :] = value.astype(bf16)
    ref[index, USED:SLAB, :] = pltpu.roll(value[0:16], 15, 0).astype(bf16)


def closure_pieces(tables, weights, work, b3, read_rows, read_mask, put):
    sel_in, sel_out = tables
    w1s, w2s, w3s, b1, b2 = weights
    patches, h1, h2, parts, flat, image = work

    def gather(g):
        halves = []
        for ip in range(2):
            rows = read_rows(64 * ip + 8 * g).reshape(48, 256)
            rows = jnp.concatenate([rows, pltpu.roll(rows, 255, 1), jnp.zeros((32, 256), f32)], axis=0)
            got = lax.dot_general(
                sel_in[...], rows.astype(bf16), (((1,), (1,)), ((), ())), preferred_element_type=f32
            )
            halves.append(got.reshape(10, 8, 128))
        both = jnp.stack(halves, axis=1).reshape(SLAB, 128).astype(bf16)
        patches[g, :, 0:128] = both[0:USED]
        patches[g, :, 128:256] = both[16:SLAB]

    def first(q, start):
        count = 3 if 4 * (start + 2) + q < ROWS1 else 2
        lhs = patches[start : start + count].reshape(count * USED, 256)
        half = jnp.dot(lhs, w1s[q], preferred_element_type=f32) + b1[...]
        out = silu_half(half)
        for g in range(count):
            store_slab(h1, 4 * (start + g) + q, out[g * USED : (g + 1) * USED])

    def second(i):
        half = b2[...]
        for di in range(2):
            for dj in range(2):
                lhs = h1[i + di : i + di + 2, 16 * dj : 16 * dj + USED, :].reshape(2 * USED, 256)
                half = half + jnp.dot(lhs, w2s[2 * di + dj], preferred_element_type=f32)
        out = silu_half(half).astype(bf16)
        m, j = i // 8, i % 8
        h2[m, :, 256 * j : 256 * j + 256] = out[0:USED]
        h2[m, :, 256 * j + 256 : 256 * j + 512] = out[USED:]

    def third(m):
        depth = 2048 if m < 4 else 512
        got = jnp.dot(h2[m, :, 0:depth], w3s[0:depth, :], preferred_element_type=f32)
        here, later = got[:, 0:128], got[:, 128:256]
        later = jnp.concatenate([later[16:USED], pltpu.roll(later[0:16], 15, 0)], axis=0)
        parts[m] = (here + later).T

    def settle(m):
        for b in range(2):
            for c in range(3):
                at = b * 64 + c * 16
                rows = parts[m, at : at + 16, :]
                if m < 4:
                    rest = parts[m + 1, b * 64 + 48 + 2 * c : b * 64 + 50 + 2 * c, :]
                    rows = rows + jnp.concatenate([jnp.zeros((14, USED), f32), rest], axis=0)
                flat[b, 48 * m + 16 * c : 48 * m + 16 * c + 16, :] = (rows + b3[c]).astype(bf16)

    def unfold(ip):
        rows = 192 + 48 * ip
        whole = jnp.dot(flat[0, 0:rows], sel_out[ip, 0], preferred_element_type=f32) + jnp.dot(
            flat[1, 0:rows], sel_out[ip, 1], preferred_element_type=f32
        )
        for m in range(4 + ip):
            for c in range(3):
                row = 64 * ip + 16 * m
                image[c, row : row + 16, :] = whole[48 * m + 16 * c : 48 * m + 16 * c + 16]

    def push():
        mask = pltpu.roll(read_mask(), 255, 1)
        xx, xy, yy = [image[c, 0:130, :] * mask for c in range(3)]

        def dx(m):
            return m[2:130, 0:TS] - m[0:128, 0:TS]

        def dy(m):
            mid = m[1:129]
            return pltpu.roll(mid, 255, 1)[:, 0:TS] - pltpu.roll(mid, 1, 1)[:, 0:TS]

        gain = (0.5 * eddy_gain) * mask[1:129, 0:TS]
        put(gain * (dx(xx) + dy(xy)), gain * (dx(xy) + dy(yy)))

    gathers = [functools.partial(gather, g) for g in range(9)]
    firsts = [functools.partial(first, q, start) for q in range(4) for start in range(0, 9, 3)]
    seconds = [functools.partial(second, i) for i in range(0, ROWS2, 2)]
    thirds = [functools.partial(third, m) for m in range(5)]
    rest = [functools.partial(settle, m) for m in range(5)]
    rest += [functools.partial(unfold, ip) for ip in range(2)] + [push]
    return gathers, firsts, seconds, thirds, rest


def run_all(*lists):
    for pieces in lists:
        for piece in pieces:
            piece()


def run_woven(gathers, firsts, seconds, thirds, rest):
    beside = {}
    for g, piece in enumerate(gathers):
        beside.setdefault(GATHER_AT[g], []).append(piece)
    for n, piece in enumerate(rest):
        beside.setdefault(REST_AT[n], []).append(piece)
    run_all(firsts)
    for i, piece in enumerate(seconds):
        piece()
        run_all(beside.get(i, []))
    run_all(thirds)


GATHER_AT = (7, 8, 9, 10, 11, 12, 13, 14, 15)
REST_AT = (0, 1, 2, 3, 4, 5, 6, 8)


KEPT = 5


def first_kernel(
    depth_h, b3_h, u, v, t, land, w1h, w2h, w3h, b1h, b2h,
    east, north, tracer, feat, act, w1s, w2s, w3s, b1r, b2r, sel_in, sel_out,
    depth, b3, ext, landx, act0, w1f, w3f, w1, w2, w3, b1, b2, pick,
    patches, h1, h2, parts, flat, image, win,
    main_out, edge_out, main_in, edge_in, res_out, res_in,
    load_sem, halo_send, halo_recv, win_send, win_recv, res_send, res_recv,
):
    level, tile = lax.axis_index("group"), lax.axis_index("tile")
    tiles = lax.axis_size("tile")
    cols = u.shape[1]
    across = cols // TS
    mesh_id = pl.DeviceIdType.MESH

    loads = [
        pltpu.make_async_copy(origin, place, load_sem.at[i])
        for i, (origin, place) in enumerate(
            (
                (w1h, w1),
                (w2h, w2),
                (w3h, w3),
                (b1h, b1),
                (b2h, b2),
                (b3_h, b3),
                (depth_h, depth),
                (u, ext.at[0, pl.ds(16, TS)]),
                (v, ext.at[1, pl.ds(16, TS)]),
                (t, ext.at[2, pl.ds(16, TS)]),
                (land, landx.at[pl.ds(16, TS)]),
            )
        )
    ]
    for load in loads:
        load.start()

    barrier = pltpu.get_barrier_semaphore()

    def greet(group, place):
        pl.semaphore_signal(barrier, inc=1, device_id=(group, place), device_id_type=mesh_id)

    @pl.when(tile > 0)
    def _():
        greet(level, tile - 1)

    @pl.when(tile < tiles - 1)
    def _():
        greet(level, tile + 1)

    @pl.when(level == 0)
    def _():
        greet(2, tile)
        greet(3, tile)

    @pl.when(level >= 2)
    def _():
        greet(0, tile)

    peers = jnp.where(tile > 0, 1, 0) + jnp.where(tile < tiles - 1, 1, 0)
    peers = peers + jnp.where(level == 0, 2, jnp.where(level == 1, 0, 1))

    for f in range(3):
        ext[f, 0:8, :] = jnp.zeros((8, cols), f32)
        ext[f, 152:160, :] = jnp.zeros((8, cols), f32)
    landx[0:8, :] = jnp.zeros((8, cols), jnp.int32)
    landx[152:160, :] = jnp.zeros((8, cols), jnp.int32)
    pl.semaphore_wait(barrier, peers)

    def halo_copy(way, f):
        src = (u, v, t, land)[f]
        rows_from, rows_to, place = ((TS - 8, 8, tile + 1), (0, 144, tile - 1))[way]
        dst = ext.at[f, pl.ds(rows_to, 8)] if f < 3 else landx.at[pl.ds(rows_to, 8)]
        return pltpu.make_async_remote_copy(
            src_ref=src.at[pl.ds(rows_from, 8)],
            dst_ref=dst,
            send_sem=halo_send.at[way, f],
            recv_sem=halo_recv.at[way, f],
            device_id=(level, place),
            device_id_type=mesh_id,
        )

    @pl.when(tile < tiles - 1)
    def _():
        for f in range(4):
            halo_copy(0, f).start()

    @pl.when(tile > 0)
    def _():
        for f in range(4):
            halo_copy(1, f).start()

    @pl.when(tile == 0)
    def _():
        for f in range(3):
            ext[f, 8:16, :] = jnp.zeros((8, cols), f32)
        landx[8:16, :] = jnp.zeros((8, cols), jnp.int32)

    @pl.when(tile == tiles - 1)
    def _():
        for f in range(3):
            ext[f, 144:152, :] = jnp.zeros((8, cols), f32)
        landx[144:152, :] = jnp.zeros((8, cols), jnp.int32)

    build_tables(sel_in, sel_out, pick)
    for load in loads[:7]:
        load.wait()
    build_weights(w1, w2, w3, b1, b2, w1f, w1s, w2s, w3f, w3s, b1r, b2r)
    lane = lax.broadcasted_iota(jnp.int32, (8, cols), 1)
    rows_all = float(tiles * TS)
    wet_mid = wet_line(depth, level, tile, lane, across)
    wet_low = wet_line(depth, level, (tile + tiles - 1) % tiles, lane, across)
    wet_high = wet_line(depth, level, (tile + 1) % tiles, lane, across)

    def rows_of(k, wet, store):
        feature_rows(
            k, tile, rows_all, wet, ext, landx, east, north, tracer, feat, act, act0, store
        )

    def inner(k, carry):
        rows_of(k, wet_mid, True)
        return carry

    for load in loads[7:]:
        load.wait()
    lax.fori_loop(1, 15, inner, 0)

    def window_copy(slot, part):
        group, place = ((2, 0), (3, 0), (3, 1))[slot]
        if part == 3:
            src, dst = edge_out.at[slot], edge_in.at[place]
        else:
            rows = pl.ds(*((16, 112), (0, 16), (128, 16))[part])
            src, dst = main_out.at[slot, :, rows], main_in.at[place, :, rows]
        return pltpu.make_async_remote_copy(
            src_ref=src,
            dst_ref=dst,
            send_sem=win_send.at[slot, part],
            recv_sem=win_recv.at[place, part],
            device_id=(group, tile),
            device_id_type=mesh_id,
        )

    @pl.when(level == 0)
    def _():
        for slot in (1, 0, 2):
            lane0 = (KEPT + slot) * TS
            main_out[slot, :, 16:128] = feat[:, 16:128, lane0 : lane0 + TS].astype(bf16)
            window_copy(slot, 0).start()


    @pl.when(tile > 0)
    def _():
        for f in range(4):
            halo_copy(0, f).wait_recv()

    @pl.when(tile < tiles - 1)
    def _():
        for f in range(4):
            halo_copy(1, f).wait_recv()

    rows_of(-1, wet_low, False)
    rows_of(0, wet_mid, True)
    rows_of(15, wet_mid, True)
    rows_of(16, wet_high, False)

    @pl.when(level == 0)
    def _():
        for slot in (1, 0, 2):
            lane0 = (KEPT + slot) * TS
            for part, rows in ((1, slice(0, 16)), (2, slice(128, 144))):
                main_out[slot, :, rows] = feat[:, rows, lane0 : lane0 + TS].astype(bf16)
                window_copy(slot, part).start()
            edge = feat[:, :, lane0 + TS : lane0 + 2 * TS].reshape(432, TS).astype(bf16)
            edge_out[slot] = lax.dot_general(
                pick[...], edge, (((1,), (1,)), ((), ())), preferred_element_type=f32
            ).astype(bf16)
            window_copy(slot, 3).start()


    def result_copy(item):
        return pltpu.make_async_remote_copy(
            src_ref=res_out.at[item],
            dst_ref=res_in.at[level - 2 + item],
            send_sem=res_send.at[item],
            recv_sem=res_recv.at[level - 2 + item],
            device_id=(0, tile),
            device_id_type=mesh_id,
        )

    tables, weights = (sel_in, sel_out), (w1s, w2s, w3s, b1r, b2r)
    work = (patches, h1, h2, parts, flat, image)

    def own_pieces(next_item, last_item):
        next_lane = pl.multiple_of(next_item * TS, TS)
        last_lane = pl.multiple_of(jnp.where(last_item < 0, 0, last_item) * TS, TS)

        def put(push_east, push_north):
            for ref, push in ((east, push_east), (north, push_north)):
                ref[:, pl.ds(last_lane, TS)] += jnp.where(last_item < 0, 0.0, push)

        return closure_pieces(
            tables, weights, work, b3,
            lambda base: feat[:, pl.ds(base, 16), pl.ds(next_lane, 2 * TS)],
            lambda: act[7:137, pl.ds(last_lane, 2 * TS)],
            put,
        )

    @pl.when(level == 0)
    def _():
        parts[...] = jnp.zeros_like(parts)
        run_all(own_pieces(0, 0)[0])

        def item_step(item, carry):
            run_woven(*own_pieces(item + 1, item - 1))
            return carry

        lax.fori_loop(0, KEPT, item_step, 0)
        run_all(own_pieces(0, KEPT - 1)[4])

    @pl.when(level >= 2)
    def _():
        def item_step(item, carry):
            for part in range(4):
                if part == 3:
                    src, dst = edge_out.at[0], edge_in.at[item]
                else:
                    rows = pl.ds(*((16, 112), (0, 16), (128, 16))[part])
                    src, dst = main_out.at[0, :, rows], main_in.at[item, :, rows]
                pltpu.make_async_remote_copy(
                    src_ref=src,
                    dst_ref=dst,
                    send_sem=win_send.at[0, part],
                    recv_sem=win_recv.at[item, part],
                    device_id=(0, tile),
                    device_id_type=mesh_id,
                ).wait_recv()
            win[:, :, 0:TS] = main_in[item].astype(f32)
            edge = lax.dot_general(
                edge_in[item], pick[...], (((0,), (0,)), ((), ())), preferred_element_type=f32
            )
            win[:, :, TS : 2 * TS] = edge.reshape(3, 144, TS)
            from0 = pl.multiple_of((KEPT + level - 2 + item) * TS, TS)

            def put(push_east, push_north):
                res_out[item, 0] = push_east
                res_out[item, 1] = push_north

            run_all(
                *closure_pieces(
                    tables, weights, work, b3,
                    lambda base: win[:, base : base + 16, :],
                    lambda: act0[7:137, pl.ds(from0, 2 * TS)],
                    put,
                )
            )
            result_copy(item).start()
            return carry

        lax.fori_loop(0, level - 1, item_step, 0)

    @pl.when(level == 0)
    def _():
        for slot in range(3):
            pltpu.make_async_remote_copy(
                src_ref=res_out.at[0],
                dst_ref=res_in.at[slot],
                send_sem=res_send.at[0],
                recv_sem=res_recv.at[slot],
                device_id=(3, tile),
                device_id_type=mesh_id,
            ).wait_recv()
            lane0 = (KEPT + slot) * TS
            east[:, lane0 : lane0 + TS] += res_in[slot, 0]
            north[:, lane0 : lane0 + TS] += res_in[slot, 1]
            for part in range(4):
                window_copy(slot, part).wait_send()

    @pl.when(level == 2)
    def _():
        result_copy(0).wait_send()

    @pl.when(level == 3)
    def _():
        result_copy(0).wait_send()
        result_copy(1).wait_send()

    @pl.when(tile < tiles - 1)
    def _():
        for f in range(4):
            halo_copy(0, f).wait_send()

    @pl.when(tile > 0)
    def _():
        for f in range(4):
            halo_copy(1, f).wait_send()


def second_kernel(
    depth_h, b3_h, east1, north1, tracer1, feat, act, w1s, w2s, w3s, b1, b2, sel_in, sel_out,
    east, north, tracer,
    depth, b3, columns, sums, patches, h1, h2, parts, flat, image,
    load_sem, tracer_sem, out_sem,
):
    level, tile = lax.axis_index("group"), lax.axis_index("tile")
    across = east1.shape[1] // TS
    tracer_copy = pltpu.make_async_copy(tracer1, tracer, tracer_sem)
    loads = [
        pltpu.make_async_copy(b3_h, b3, load_sem.at[0]),
        pltpu.make_async_copy(depth_h, depth, load_sem.at[1]),
    ]
    for load in loads:
        load.start()
    tracer_copy.start()
    sums[0] = east1[...]
    sums[1] = north1[...]
    for load in loads:
        load.wait()

    def block_copy(ty, which):
        lanes = pl.ds(pl.multiple_of(ty * TS, TS), TS)
        return pltpu.make_async_copy(
            sums.at[which, :, lanes], (east, north)[which].at[:, lanes], out_sem.at[ty, which]
        )

    def send(ty):
        for which in range(2):
            block_copy(ty, which).start()

    count = jnp.int32(0)
    for ty in range(across):
        mine = (level > 0) & (depth[tile * across + ty] > level)
        columns[count] = jnp.int32(ty)
        count = count + mine.astype(jnp.int32)

        @pl.when(jnp.logical_not(mine))
        def _():
            send(ty)

    def own_pieces(next_item, last_item):
        next_lane = pl.multiple_of(columns[next_item] * TS, TS)
        last_lane = pl.multiple_of(columns[jnp.maximum(last_item, 0)] * TS, TS)

        def put(push_east, push_north):
            for which, push in ((0, push_east), (1, push_north)):
                sums[which, :, pl.ds(last_lane, TS)] += jnp.where(last_item < 0, 0.0, push)

        return closure_pieces(
            (sel_in, sel_out), (w1s, w2s, w3s, b1, b2), (patches, h1, h2, parts, flat, image), b3,
            lambda base: feat[:, pl.ds(base, 16), pl.ds(next_lane, 2 * TS)],
            lambda: act[7:137, pl.ds(last_lane, 2 * TS)],
            put,
        )

    @pl.when(count > 0)
    def _():
        parts[...] = jnp.zeros_like(parts)
        run_all(own_pieces(0, 0)[0])

        def item_step(item, carry):
            run_woven(*own_pieces(jnp.minimum(item + 1, count - 1), item - 1))

            @pl.when(item > 0)
            def _():
                send(columns[item - 1])

            return carry

        lax.fori_loop(0, count, item_step, 0)
        run_all(own_pieces(0, count - 1)[4])
        send(columns[count - 1])

    def drain(ty, carry):
        for which in range(2):
            block_copy(ty, which).wait()
        return carry

    lax.fori_loop(0, across, drain, 0)
    tracer_copy.wait()


def body(u, v, t, land, depth, conv_one, bias_one, conv_two, bias_two, conv_three, bias_three):
    levels, rows, cols = u.shape
    vmem = pl.BlockSpec(memory_space=pltpu.VMEM)
    hbm = pl.BlockSpec(memory_space=pltpu.HBM)
    wide = cols + TS
    across = cols // TS
    plane = jax.ShapeDtypeStruct((rows, cols), f32)
    work = [
        pltpu.VMEM((9, USED, 256), bf16),
        pltpu.VMEM((ROWS1 + 1, SLAB, 256), bf16),
        pltpu.VMEM((5, USED, 2048), bf16),
        pltpu.VMEM((5, TS, USED), f32),
        pltpu.VMEM((2, 240, USED), bf16),
        pltpu.VMEM((3, 144, 256), f32),
    ]
    def stay(x):
        return pltpu.with_memory_space_constraint(x, pltpu.HBM)

    east1, north1, tracer1, feat, act, w1s, w2s, w3s, b1r, b2r, sel_in, sel_out = pl.pallas_call(
        first_kernel,
        out_shape=[plane] * 3
        + [
            jax.ShapeDtypeStruct((3, 144, wide), f32),
            jax.ShapeDtypeStruct((144, wide), f32),
            jax.ShapeDtypeStruct((4, 256, 256), bf16),
            jax.ShapeDtypeStruct((4, 256, 256), bf16),
            jax.ShapeDtypeStruct((2048, 256), bf16),
            jax.ShapeDtypeStruct((1, 256), f32),
            jax.ShapeDtypeStruct((1, 256), f32),
            jax.ShapeDtypeStruct((80, 256), bf16),
            jax.ShapeDtypeStruct((2, 2, USED, 256), bf16),
        ],
        in_specs=[hbm] * 11,
        out_specs=[vmem] * 12,
        scratch_shapes=[
            pltpu.SMEM(depth.shape, jnp.int32),
            pltpu.SMEM((3,), f32),
            pltpu.VMEM((3, 160, cols), f32),
            pltpu.VMEM((160, cols), jnp.int32),
            pltpu.VMEM((144, wide), f32),
            pltpu.VMEM((4, 256, 256), f32),
            pltpu.VMEM((64, 256), f32),
            pltpu.VMEM((3, 3, 3, 64), bf16),
            pltpu.VMEM((3, 3, 64, 64), bf16),
            pltpu.VMEM((3, 3, 3, 64), bf16),
            pltpu.VMEM((1, 64), f32),
            pltpu.VMEM((1, 64), f32),
            pltpu.VMEM((16, TS), bf16),
        ]
        + work
        + [
            pltpu.VMEM((3, 144, 2 * TS), f32),
            pltpu.VMEM((3, 3, 144, TS), bf16),
            pltpu.VMEM((3, 16, 432), bf16),
            pltpu.VMEM((2, 3, 144, TS), bf16),
            pltpu.VMEM((2, 16, 432), bf16),
            pltpu.VMEM((2, 2, TS, TS), f32),
            pltpu.VMEM((3, 2, TS, TS), f32),
            pltpu.SemaphoreType.DMA((11,)),
            pltpu.SemaphoreType.DMA((2, 4)),
            pltpu.SemaphoreType.DMA((2, 4)),
            pltpu.SemaphoreType.DMA((3, 4)),
            pltpu.SemaphoreType.DMA((2, 4)),
            pltpu.SemaphoreType.DMA((2,)),
            pltpu.SemaphoreType.DMA((3,)),
        ],
        compiler_params=pltpu.CompilerParams(
            vmem_limit_bytes=40 * 2**20, collective_id=0, has_side_effects=True
        ),
        name="first",
    )(
        stay(depth), stay(bias_three), stay(u[0]), stay(v[0]), stay(t[0]), stay(land),
        stay(conv_one.transpose(1, 2, 3, 0)), stay(conv_two.transpose(2, 3, 0, 1)),
        stay(conv_three.transpose(0, 2, 3, 1)), stay(bias_one[None]), stay(bias_two[None]),
    )
    east, north, tracer = pl.pallas_call(
        second_kernel,
        out_shape=[plane] * 3,
        in_specs=[hbm] * 2 + [vmem] * 12,
        out_specs=[hbm] * 3,
        scratch_shapes=[
            pltpu.SMEM(depth.shape, jnp.int32),
            pltpu.SMEM((3,), f32),
            pltpu.SMEM((across,), jnp.int32),
            pltpu.VMEM((2, rows, cols), f32),
        ]
        + work
        + [pltpu.SemaphoreType.DMA((2,)), pltpu.SemaphoreType.DMA, pltpu.SemaphoreType.DMA((across, 2))],
        compiler_params=pltpu.CompilerParams(vmem_limit_bytes=40 * 2**20),
        name="second",
    )(
        stay(depth), stay(bias_three), east1, north1, tracer1, feat, act, w1s, w2s, w3s, b1r, b2r,
        sel_in, sel_out,
    )
    return east[None], north[None], tracer[None]


def solution(mesh):
    field = P("group", "tile", None)
    in_specs = (field, field, field, P("tile", None)) + (P(),) * 7
    return jax.shard_map(
        body, mesh=mesh, in_specs=in_specs, out_specs=(field,) * 3, check_vma=False
    )
```

```python
import functools

import jax
import jax.numpy as jnp
from jax import lax
from jax.experimental import pallas as pl
from jax.experimental.pallas import tpu as pltpu
from jax.sharding import PartitionSpec as P

time_step = 0.1
viscosity = 0.5
diffusivity = 0.5
eddy_gain = 0.5
coriolis_base = 0.2
coriolis_slope = 0.6

bf16 = jnp.bfloat16
f32 = jnp.float32

TS = 128
HALO = 5
ROWS1, ROWS2 = 35, 34
SLAB = 160
USED = 144


def build_tables(sel_in, sel_out, pick):
    row = lax.broadcasted_iota(jnp.int32, (80, 256), 0)
    col = lax.broadcasted_iota(jnp.int32, (80, 256), 1)
    sel_in[...] = (col == 2 * (9 * (row % 8) + row // 8)).astype(f32).astype(bf16)
    row = lax.broadcasted_iota(jnp.int32, (USED, 256), 0)
    col = lax.broadcasted_iota(jnp.int32, (USED, 256), 1)
    place = 2 * (9 * (row % 8) + row // 16)
    inside = place + 1 < 130
    for ip in range(2):
        for b in range(2):
            hit = inside & ((row % 16) // 8 == ip) & (col == (place + b + 255) % 256)
            sel_out[ip, b] = hit.astype(f32).astype(bf16)
    row = lax.broadcasted_iota(jnp.int32, (16, TS), 0)
    col = lax.broadcasted_iota(jnp.int32, (16, TS), 1)
    pick[...] = (row == col).astype(f32).astype(bf16)


def taps():
    for outer in range(2):
        for inner in range(2):
            for out in range(2):
                k = 2 * outer + inner - out
                if 0 <= k < 3:
                    yield outer, inner, out, k


def build_weights(w1, w2, w3, b1, b2, w1f, w1s, w2s, w3f, w3s, b1r, b2r):
    w1f[...] = jnp.zeros_like(w1f)
    for c in range(3):
        for kx in range(3):
            line = 0.5 * w1[c, kx].astype(f32)
            for q in range(4):
                for dj, dy, b, ky in taps():
                    for a in range(2):
                        row = dj * 128 + dy * 48 + c * 16 + 4 + 2 * q + a + kx
                        lane = (a * 2 + b) * 64
                        w1f[q, row : row + 1, lane : lane + 64] = line[ky : ky + 1]
    w1s[...] = w1f[...].astype(bf16)
    w2s[...] = jnp.zeros_like(w2s)
    for kx in range(3):
        for ky in range(3):
            block = (0.5 * w2[kx, ky].astype(f32)).T.astype(bf16)
            for di, ai, ao, kx_here in taps():
                for dj, bi, bo, ky_here in taps():
                    if (kx, ky) == (kx_here, ky_here):
                        row = (ai * 2 + bi) * 64
                        lane = (ao * 2 + bo) * 64
                        w2s[di * 2 + dj, row : row + 64, lane : lane + 64] = block
    w3f[...] = jnp.zeros_like(w3f)
    for c in range(3):
        for kx in range(3):
            line = w3[c, kx].astype(f32)
            for di, ai, ao, kx_here in taps():
                if kx != kx_here:
                    continue
                for dj, bi, bo, ky in taps():
                    lane = (ai * 2 + bi) * 64
                    row = (di * 2 + dj) * 16 + bo * 6 + c * 2 + ao
                    w3f[row : row + 1, lane : lane + 64] = line[ky : ky + 1]
    turned = w3f[...].T.astype(bf16)
    row = lax.broadcasted_iota(jnp.int32, (64, 256), 0)
    col = lax.broadcasted_iota(jnp.int32, (64, 256), 1)
    part = row % 16
    di, dj = row // 32, (row // 16) % 2
    b, c, a = part // 6, (part % 6) // 2, part % 2
    for j in range(8):
        into = jnp.where(j - di >= 0, c * 16 + 2 * (j - di), 48 + 2 * c)
        hit = (part < 12) & (col == dj * 128 + b * 64 + into + a)
        spread = jnp.dot(turned, hit.astype(f32).astype(bf16), preferred_element_type=f32)
        w3s[256 * j : 256 * j + 256, :] = spread.astype(bf16)
    for j in range(4):
        b1r[:, 64 * j : 64 * j + 64] = 0.5 * b1[...]
        b2r[:, 64 * j : 64 * j + 64] = 0.5 * b2[...]


def wet_line(depth, level, tile_row, lane, across):
    line = jnp.zeros(lane.shape, f32)
    for ty in range(across):
        wet = (depth[tile_row * across + ty] > level).astype(f32)
        line = jnp.where(lane // TS == ty, wet, line)
    return line


def feature_rows(k, tile, rows_all, wet, ext, landx, east, north, tracer, feat, act, act0, store):
    cols = landx.shape[1]
    lane = lax.broadcasted_iota(jnp.int32, (8, cols), 1)
    row = lax.broadcasted_iota(jnp.int32, (8, cols), 0)
    zeros = jnp.zeros((8, TS), f32)

    def west(x):
        return jnp.where(lane == 0, 0.0, pltpu.roll(x, 1, 1))

    def east_of(x):
        return jnp.where(lane == cols - 1, 0.0, pltpu.roll(x, cols - 1, 1))

    base = 8 * k + 16
    water = jnp.where(landx[base : base + 8, :] == 1, 1.0, 0.0)
    active = water * wet
    mid = [ext[f, base : base + 8, :] for f in range(3)]
    up = [ext[f, base - 1 : base + 7, :] for f in range(3)]
    down = [ext[f, base + 1 : base + 9, :] for f in range(3)]
    left = [west(x) for x in mid]
    right = [east_of(x) for x in mid]
    lap = [down[f] + up[f] + right[f] + left[f] - 4.0 * mid[f] for f in range(3)]
    grad_east = 0.5 * (down[2] - up[2])
    grad_north = 0.5 * (right[2] - left[2])
    place = (tile * TS + 8 * k + row).astype(f32)
    coriolis = coriolis_base + coriolis_slope * (place + 0.5) / rows_all
    step = time_step * active
    new_east = mid[0] + step * (coriolis * mid[1] - grad_east + viscosity * lap[0])
    new_north = mid[1] + step * (-coriolis * mid[0] - grad_north + viscosity * lap[1])
    new_tracer = mid[2] + step * (
        -(mid[0] * grad_east + mid[1] * grad_north) + diffusivity * lap[2]
    )
    if store:
        at = 8 * k
        east[pl.ds(at, 8), :] = new_east
        north[pl.ds(at, 8), :] = new_north
        tracer[pl.ds(at, 8), :] = new_tracer
    q = 8 * k + 8
    for c, new in enumerate((new_east, new_north, new_tracer)):
        wide = jnp.concatenate([new * active, zeros], axis=1)
        feat[c, pl.ds(q, 8), :] = pltpu.roll(wide, 4, 1)
    act[pl.ds(q, 8), :] = pltpu.roll(jnp.concatenate([active, zeros], axis=1), 1, 1)
    act0[pl.ds(q, 8), :] = pltpu.roll(jnp.concatenate([water, zeros], axis=1), 1, 1)


def silu_half(half):
    return half + half * jnp.tanh(half)


def store_slab(ref, index, value):
    ref[index, 0:USED, :] = value.astype(bf16)
    ref[index, USED:SLAB, :] = pltpu.roll(value[0:16], 15, 0).astype(bf16)


def closure_pieces(tables, weights, work, b3, read_rows, read_mask, put):
    sel_in, sel_out = tables
    w1s, w2s, w3s, b1, b2 = weights
    patches, h1, h2, parts, flat, image = work

    def gather(g):
        halves = []
        for ip in range(2):
            rows = read_rows(64 * ip + 8 * g).reshape(48, 256)
            rows = jnp.concatenate([rows, pltpu.roll(rows, 255, 1), jnp.zeros((32, 256), f32)], axis=0)
            got = lax.dot_general(
                sel_in[...], rows.astype(bf16), (((1,), (1,)), ((), ())), preferred_element_type=f32
            )
            halves.append(got.reshape(10, 8, 128))
        both = jnp.stack(halves, axis=1).reshape(SLAB, 128).astype(bf16)
        patches[g, :, 0:128] = both[0:USED]
        patches[g, :, 128:256] = both[16:SLAB]

    def first(q, start):
        count = 3 if 4 * (start + 2) + q < ROWS1 else 2
        lhs = patches[start : start + count].reshape(count * USED, 256)
        half = jnp.dot(lhs, w1s[q], preferred_element_type=f32) + b1[...]
        out = silu_half(half)
        for g in range(count):
            store_slab(h1, 4 * (start + g) + q, out[g * USED : (g + 1) * USED])

    def second(i):
        half = b2[...]
        for di in range(2):
            for dj in range(2):
                lhs = h1[i + di : i + di + 2, 16 * dj : 16 * dj + USED, :].reshape(2 * USED, 256)
                half = half + jnp.dot(lhs, w2s[2 * di + dj], preferred_element_type=f32)
        out = silu_half(half).astype(bf16)
        m, j = i // 8, i % 8
        h2[m, :, 256 * j : 256 * j + 256] = out[0:USED]
        h2[m, :, 256 * j + 256 : 256 * j + 512] = out[USED:]

    def third(m):
        depth = 2048 if m < 4 else 512
        got = jnp.dot(h2[m, :, 0:depth], w3s[0:depth, :], preferred_element_type=f32)
        here, later = got[:, 0:128], got[:, 128:256]
        later = jnp.concatenate([later[16:USED], pltpu.roll(later[0:16], 15, 0)], axis=0)
        parts[m] = (here + later).T

    def settle(m):
        for b in range(2):
            for c in range(3):
                at = b * 64 + c * 16
                rows = parts[m, at : at + 16, :]
                if m < 4:
                    rest = parts[m + 1, b * 64 + 48 + 2 * c : b * 64 + 50 + 2 * c, :]
                    rows = rows + jnp.concatenate([jnp.zeros((14, USED), f32), rest], axis=0)
                flat[b, 48 * m + 16 * c : 48 * m + 16 * c + 16, :] = (rows + b3[c]).astype(bf16)

    def unfold(ip):
        rows = 192 + 48 * ip
        whole = jnp.dot(flat[0, 0:rows], sel_out[ip, 0], preferred_element_type=f32) + jnp.dot(
            flat[1, 0:rows], sel_out[ip, 1], preferred_element_type=f32
        )
        for m in range(4 + ip):
            for c in range(3):
                row = 64 * ip + 16 * m
                image[c, row : row + 16, :] = whole[48 * m + 16 * c : 48 * m + 16 * c + 16]

    def push():
        mask = pltpu.roll(read_mask(), 255, 1)
        xx, xy, yy = [image[c, 0:130, :] * mask for c in range(3)]

        def dx(m):
            return m[2:130, 0:TS] - m[0:128, 0:TS]

        def dy(m):
            mid = m[1:129]
            return pltpu.roll(mid, 255, 1)[:, 0:TS] - pltpu.roll(mid, 1, 1)[:, 0:TS]

        gain = (0.5 * eddy_gain) * mask[1:129, 0:TS]
        put(gain * (dx(xx) + dy(xy)), gain * (dx(xy) + dy(yy)))

    gathers = [functools.partial(gather, g) for g in range(9)]
    firsts = [functools.partial(first, q, start) for q in range(4) for start in range(0, 9, 3)]
    seconds = [functools.partial(second, i) for i in range(0, ROWS2, 2)]
    thirds = [functools.partial(third, m) for m in range(5)]
    rest = [functools.partial(settle, m) for m in range(5)]
    rest += [functools.partial(unfold, ip) for ip in range(2)] + [push]
    return gathers, firsts, seconds, thirds, rest


def run_all(*lists):
    for pieces in lists:
        for piece in pieces:
            piece()


def run_woven(gathers, firsts, seconds, thirds, rest):
    beside = {}
    for g, piece in enumerate(gathers):
        beside.setdefault(GATHER_AT[g], []).append(piece)
    for n, piece in enumerate(rest):
        beside.setdefault(REST_AT[n], []).append(piece)
    run_all(firsts)
    for i, piece in enumerate(seconds):
        piece()
        run_all(beside.get(i, []))
    run_all(thirds)


GATHER_AT = (7, 8, 9, 10, 11, 12, 13, 14, 15)
REST_AT = (0, 1, 2, 3, 4, 5, 6, 8)


KEPT = 5


def first_kernel(
    depth_h, b3_h, u, v, t, land, w1h, w2h, w3h, b1h, b2h,
    east, north, tracer, feat, act, w1s, w2s, w3s, b1r, b2r, sel_in, sel_out,
    depth, b3, ext, landx, act0, w1f, w3f, w1, w2, w3, b1, b2, pick,
    patches, h1, h2, parts, flat, image, win,
    main_out, edge_out, main_in, edge_in, res_out, res_in,
    load_sem, halo_send, halo_recv, win_send, win_recv, res_send, res_recv,
):
    level, tile = lax.axis_index("group"), lax.axis_index("tile")
    tiles = lax.axis_size("tile")
    cols = u.shape[1]
    across = cols // TS
    mesh_id = pl.DeviceIdType.MESH

    loads = [
        pltpu.make_async_copy(origin, place, load_sem.at[i])
        for i, (origin, place) in enumerate(
            (
                (w1h, w1),
                (w2h, w2),
                (w3h, w3),
                (b1h, b1),
                (b2h, b2),
                (b3_h, b3),
                (depth_h, depth),
                (u, ext.at[0, pl.ds(16, TS)]),
                (v, ext.at[1, pl.ds(16, TS)]),
                (t, ext.at[2, pl.ds(16, TS)]),
                (land, landx.at[pl.ds(16, TS)]),
            )
        )
    ]
    for load in loads:
        load.start()

    barrier = pltpu.get_barrier_semaphore()

    def greet(group, place):
        pl.semaphore_signal(barrier, inc=1, device_id=(group, place), device_id_type=mesh_id)

    @pl.when(tile > 0)
    def _():
        greet(level, tile - 1)

    @pl.when(tile < tiles - 1)
    def _():
        greet(level, tile + 1)

    @pl.when(level == 0)
    def _():
        greet(2, tile)
        greet(3, tile)

    @pl.when(level >= 2)
    def _():
        greet(0, tile)

    peers = jnp.where(tile > 0, 1, 0) + jnp.where(tile < tiles - 1, 1, 0)
    peers = peers + jnp.where(level == 0, 2, jnp.where(level == 1, 0, 1))

    for f in range(3):
        ext[f, 0:8, :] = jnp.zeros((8, cols), f32)
        ext[f, 152:160, :] = jnp.zeros((8, cols), f32)
    landx[0:8, :] = jnp.zeros((8, cols), jnp.int32)
    landx[152:160, :] = jnp.zeros((8, cols), jnp.int32)
    pl.semaphore_wait(barrier, peers)

    def halo_copy(way, f):
        src = (u, v, t, land)[f]
        rows_from, rows_to, place = ((TS - 8, 8, tile + 1), (0, 144, tile - 1))[way]
        dst = ext.at[f, pl.ds(rows_to, 8)] if f < 3 else landx.at[pl.ds(rows_to, 8)]
        return pltpu.make_async_remote_copy(
            src_ref=src.at[pl.ds(rows_from, 8)],
            dst_ref=dst,
            send_sem=halo_send.at[way, f],
            recv_sem=halo_recv.at[way, f],
            device_id=(level, place),
            device_id_type=mesh_id,
        )

    @pl.when(tile < tiles - 1)
    def _():
        for f in range(4):
            halo_copy(0, f).start()

    @pl.when(tile > 0)
    def _():
        for f in range(4):
            halo_copy(1, f).start()

    @pl.when(tile == 0)
    def _():
        for f in range(3):
            ext[f, 8:16, :] = jnp.zeros((8, cols), f32)
        landx[8:16, :] = jnp.zeros((8, cols), jnp.int32)

    @pl.when(tile == tiles - 1)
    def _():
        for f in range(3):
            ext[f, 144:152, :] = jnp.zeros((8, cols), f32)
        landx[144:152, :] = jnp.zeros((8, cols), jnp.int32)

    build_tables(sel_in, sel_out, pick)
    for load in loads[5:7]:
        load.wait()
    lane = lax.broadcasted_iota(jnp.int32, (8, cols), 1)
    rows_all = float(tiles * TS)
    wet_mid = wet_line(depth, level, tile, lane, across)
    wet_low = wet_line(depth, level, (tile + tiles - 1) % tiles, lane, across)
    wet_high = wet_line(depth, level, (tile + 1) % tiles, lane, across)

    def rows_of(k, wet, store):
        feature_rows(
            k, tile, rows_all, wet, ext, landx, east, north, tracer, feat, act, act0, store
        )

    for load in loads[7:]:
        load.wait()
    for k in range(1, 15):
        rows_of(k, wet_mid, True)

    def window_copy(slot, part):
        group, place = ((2, 0), (3, 0), (3, 1))[slot]
        if part == 3:
            src, dst = edge_out.at[slot], edge_in.at[place]
        else:
            rows = pl.ds(*((16, 112), (0, 16), (128, 16))[part])
            src, dst = main_out.at[slot, :, rows], main_in.at[place, :, rows]
        return pltpu.make_async_remote_copy(
            src_ref=src,
            dst_ref=dst,
            send_sem=win_send.at[slot, part],
            recv_sem=win_recv.at[place, part],
            device_id=(group, tile),
            device_id_type=mesh_id,
        )

    @pl.when(level == 0)
    def _():
        for slot in (1, 0, 2):
            lane0 = (KEPT + slot) * TS
            main_out[slot, :, 16:128] = feat[:, 16:128, lane0 : lane0 + TS].astype(bf16)
            window_copy(slot, 0).start()

    for load in loads[:5]:
        load.wait()
    build_weights(w1, w2, w3, b1, b2, w1f, w1s, w2s, w3f, w3s, b1r, b2r)


    @pl.when(tile > 0)
    def _():
        for f in range(4):
            halo_copy(0, f).wait_recv()

    @pl.when(tile < tiles - 1)
    def _():
        for f in range(4):
            halo_copy(1, f).wait_recv()

    rows_of(-1, wet_low, False)
    rows_of(0, wet_mid, True)
    rows_of(15, wet_mid, True)
    rows_of(16, wet_high, False)

    @pl.when(level == 0)
    def _():
        for slot in (1, 0, 2):
            lane0 = (KEPT + slot) * TS
            for part, rows in ((1, slice(0, 16)), (2, slice(128, 144))):
                main_out[slot, :, rows] = feat[:, rows, lane0 : lane0 + TS].astype(bf16)
                window_copy(slot, part).start()
            edge = feat[:, :, lane0 + TS : lane0 + 2 * TS].reshape(432, TS).astype(bf16)
            edge_out[slot] = lax.dot_general(
                pick[...], edge, (((1,), (1,)), ((), ())), preferred_element_type=f32
            ).astype(bf16)
            window_copy(slot, 3).start()


    def result_copy(item):
        return pltpu.make_async_remote_copy(
            src_ref=res_out.at[item],
            dst_ref=res_in.at[level - 2 + item],
            send_sem=res_send.at[item],
            recv_sem=res_recv.at[level - 2 + item],
            device_id=(0, tile),
            device_id_type=mesh_id,
        )

    tables, weights = (sel_in, sel_out), (w1s, w2s, w3s, b1r, b2r)
    work = (patches, h1, h2, parts, flat, image)

    def own_pieces(next_item, last_item):
        next_lane = pl.multiple_of(next_item * TS, TS)
        last_lane = pl.multiple_of(jnp.where(last_item < 0, 0, last_item) * TS, TS)

        def put(push_east, push_north):
            for ref, push in ((east, push_east), (north, push_north)):
                ref[:, pl.ds(last_lane, TS)] += jnp.where(last_item < 0, 0.0, push)

        return closure_pieces(
            tables, weights, work, b3,
            lambda base: feat[:, pl.ds(base, 16), pl.ds(next_lane, 2 * TS)],
            lambda: act[7:137, pl.ds(last_lane, 2 * TS)],
            put,
        )

    @pl.when(level == 0)
    def _():
        parts[...] = jnp.zeros_like(parts)
        run_all(own_pieces(0, 0)[0])

        def item_step(item, carry):
            run_woven(*own_pieces(item + 1, item - 1))
            return carry

        lax.fori_loop(0, KEPT, item_step, 0)
        run_all(own_pieces(0, KEPT - 1)[4])

    @pl.when(level >= 2)
    def _():
        def item_step(item, carry):
            for part in range(4):
                if part == 3:
                    src, dst = edge_out.at[0], edge_in.at[item]
                else:
                    rows = pl.ds(*((16, 112), (0, 16), (128, 16))[part])
                    src, dst = main_out.at[0, :, rows], main_in.at[item, :, rows]
                pltpu.make_async_remote_copy(
                    src_ref=src,
                    dst_ref=dst,
                    send_sem=win_send.at[0, part],
                    recv_sem=win_recv.at[item, part],
                    device_id=(0, tile),
                    device_id_type=mesh_id,
                ).wait_recv()
            win[:, :, 0:TS] = main_in[item].astype(f32)
            edge = lax.dot_general(
                edge_in[item], pick[...], (((0,), (0,)), ((), ())), preferred_element_type=f32
            )
            win[:, :, TS : 2 * TS] = edge.reshape(3, 144, TS)
            from0 = pl.multiple_of((KEPT + level - 2 + item) * TS, TS)

            def put(push_east, push_north):
                res_out[item, 0] = push_east.astype(bf16)
                res_out[item, 1] = push_north.astype(bf16)

            run_all(
                *closure_pieces(
                    tables, weights, work, b3,
                    lambda base: win[:, base : base + 16, :],
                    lambda: act0[7:137, pl.ds(from0, 2 * TS)],
                    put,
                )
            )
            result_copy(item).start()
            return carry

        lax.fori_loop(0, level - 1, item_step, 0)

    @pl.when(level == 0)
    def _():
        for slot in range(3):
            pltpu.make_async_remote_copy(
                src_ref=res_out.at[0],
                dst_ref=res_in.at[slot],
                send_sem=res_send.at[0],
                recv_sem=res_recv.at[slot],
                device_id=(3, tile),
                device_id_type=mesh_id,
            ).wait_recv()
            lane0 = (KEPT + slot) * TS
            east[:, lane0 : lane0 + TS] += res_in[slot, 0].astype(f32)
            north[:, lane0 : lane0 + TS] += res_in[slot, 1].astype(f32)
            for part in range(4):
                window_copy(slot, part).wait_send()

    @pl.when(level == 2)
    def _():
        result_copy(0).wait_send()

    @pl.when(level == 3)
    def _():
        result_copy(0).wait_send()
        result_copy(1).wait_send()

    @pl.when(tile < tiles - 1)
    def _():
        for f in range(4):
            halo_copy(0, f).wait_send()

    @pl.when(tile > 0)
    def _():
        for f in range(4):
            halo_copy(1, f).wait_send()


def second_kernel(
    depth_h, b3_h, east1, north1, tracer1, feat, act, w1s, w2s, w3s, b1, b2, sel_in, sel_out,
    east, north, tracer,
    depth, b3, columns, sums, patches, h1, h2, parts, flat, image,
    load_sem, tracer_sem, out_sem,
):
    level, tile = lax.axis_index("group"), lax.axis_index("tile")
    across = east1.shape[1] // TS
    tracer_copy = pltpu.make_async_copy(tracer1, tracer, tracer_sem)
    loads = [
        pltpu.make_async_copy(b3_h, b3, load_sem.at[0]),
        pltpu.make_async_copy(depth_h, depth, load_sem.at[1]),
    ]
    for load in loads:
        load.start()
    tracer_copy.start()
    sums[0] = east1[...]
    sums[1] = north1[...]
    for load in loads:
        load.wait()

    def block_copy(ty, which):
        lanes = pl.ds(pl.multiple_of(ty * TS, TS), TS)
        return pltpu.make_async_copy(
            sums.at[which, :, lanes], (east, north)[which].at[:, lanes], out_sem.at[ty, which]
        )

    def send(ty):
        for which in range(2):
            block_copy(ty, which).start()

    count = jnp.int32(0)
    for ty in range(across):
        mine = (level > 0) & (depth[tile * across + ty] > level)
        columns[count] = jnp.int32(ty)
        count = count + mine.astype(jnp.int32)

        @pl.when(jnp.logical_not(mine))
        def _():
            send(ty)

    def own_pieces(next_item, last_item):
        next_lane = pl.multiple_of(columns[next_item] * TS, TS)
        last_lane = pl.multiple_of(columns[jnp.maximum(last_item, 0)] * TS, TS)

        def put(push_east, push_north):
            for which, push in ((0, push_east), (1, push_north)):
                sums[which, :, pl.ds(last_lane, TS)] += jnp.where(last_item < 0, 0.0, push)

        return closure_pieces(
            (sel_in, sel_out), (w1s, w2s, w3s, b1, b2), (patches, h1, h2, parts, flat, image), b3,
            lambda base: feat[:, pl.ds(base, 16), pl.ds(next_lane, 2 * TS)],
            lambda: act[7:137, pl.ds(last_lane, 2 * TS)],
            put,
        )

    @pl.when(count > 0)
    def _():
        parts[...] = jnp.zeros_like(parts)
        run_all(own_pieces(0, 0)[0])

        def item_step(item, carry):
            run_woven(*own_pieces(jnp.minimum(item + 1, count - 1), item - 1))

            @pl.when(item > 0)
            def _():
                send(columns[item - 1])

            return carry

        lax.fori_loop(0, count, item_step, 0)
        run_all(own_pieces(0, count - 1)[4])
        send(columns[count - 1])

    def drain(ty, carry):
        for which in range(2):
            block_copy(ty, which).wait()
        return carry

    lax.fori_loop(0, across, drain, 0)
    tracer_copy.wait()


def body(u, v, t, land, depth, conv_one, bias_one, conv_two, bias_two, conv_three, bias_three):
    levels, rows, cols = u.shape
    vmem = pl.BlockSpec(memory_space=pltpu.VMEM)
    hbm = pl.BlockSpec(memory_space=pltpu.HBM)
    wide = cols + TS
    across = cols // TS
    plane = jax.ShapeDtypeStruct((rows, cols), f32)
    work = [
        pltpu.VMEM((9, USED, 256), bf16),
        pltpu.VMEM((ROWS1 + 1, SLAB, 256), bf16),
        pltpu.VMEM((5, USED, 2048), bf16),
        pltpu.VMEM((5, TS, USED), f32),
        pltpu.VMEM((2, 240, USED), bf16),
        pltpu.VMEM((3, 144, 256), f32),
    ]
    def stay(x):
        return pltpu.with_memory_space_constraint(x, pltpu.HBM)

    east1, north1, tracer1, feat, act, w1s, w2s, w3s, b1r, b2r, sel_in, sel_out = pl.pallas_call(
        first_kernel,
        out_shape=[plane] * 3
        + [
            jax.ShapeDtypeStruct((3, 144, wide), f32),
            jax.ShapeDtypeStruct((144, wide), f32),
            jax.ShapeDtypeStruct((4, 256, 256), bf16),
            jax.ShapeDtypeStruct((4, 256, 256), bf16),
            jax.ShapeDtypeStruct((2048, 256), bf16),
            jax.ShapeDtypeStruct((1, 256), f32),
            jax.ShapeDtypeStruct((1, 256), f32),
            jax.ShapeDtypeStruct((80, 256), bf16),
            jax.ShapeDtypeStruct((2, 2, USED, 256), bf16),
        ],
        in_specs=[hbm] * 11,
        out_specs=[vmem] * 12,
        scratch_shapes=[
            pltpu.SMEM(depth.shape, jnp.int32),
            pltpu.SMEM((3,), f32),
            pltpu.VMEM((3, 160, cols), f32),
            pltpu.VMEM((160, cols), jnp.int32),
            pltpu.VMEM((144, wide), f32),
            pltpu.VMEM((4, 256, 256), f32),
            pltpu.VMEM((64, 256), f32),
            pltpu.VMEM((3, 3, 3, 64), bf16),
            pltpu.VMEM((3, 3, 64, 64), bf16),
            pltpu.VMEM((3, 3, 3, 64), bf16),
            pltpu.VMEM((1, 64), f32),
            pltpu.VMEM((1, 64), f32),
            pltpu.VMEM((16, TS), bf16),
        ]
        + work
        + [
            pltpu.VMEM((3, 144, 2 * TS), f32),
            pltpu.VMEM((3, 3, 144, TS), bf16),
            pltpu.VMEM((3, 16, 432), bf16),
            pltpu.VMEM((2, 3, 144, TS), bf16),
            pltpu.VMEM((2, 16, 432), bf16),
            pltpu.VMEM((2, 2, TS, TS), bf16),
            pltpu.VMEM((3, 2, TS, TS), bf16),
            pltpu.SemaphoreType.DMA((11,)),
            pltpu.SemaphoreType.DMA((2, 4)),
            pltpu.SemaphoreType.DMA((2, 4)),
            pltpu.SemaphoreType.DMA((3, 4)),
            pltpu.SemaphoreType.DMA((2, 4)),
            pltpu.SemaphoreType.DMA((2,)),
            pltpu.SemaphoreType.DMA((3,)),
        ],
        compiler_params=pltpu.CompilerParams(
            vmem_limit_bytes=40 * 2**20, collective_id=0, has_side_effects=True
        ),
        name="first",
    )(
        stay(depth), stay(bias_three), stay(u[0]), stay(v[0]), stay(t[0]), stay(land),
        stay(conv_one.transpose(1, 2, 3, 0)), stay(conv_two.transpose(2, 3, 0, 1)),
        stay(conv_three.transpose(0, 2, 3, 1)), stay(bias_one[None]), stay(bias_two[None]),
    )
    east, north, tracer = pl.pallas_call(
        second_kernel,
        out_shape=[plane] * 3,
        in_specs=[hbm] * 2 + [vmem] * 12,
        out_specs=[hbm] * 3,
        scratch_shapes=[
            pltpu.SMEM(depth.shape, jnp.int32),
            pltpu.SMEM((3,), f32),
            pltpu.SMEM((across,), jnp.int32),
            pltpu.VMEM((2, rows, cols), f32),
        ]
        + work
        + [pltpu.SemaphoreType.DMA((2,)), pltpu.SemaphoreType.DMA, pltpu.SemaphoreType.DMA((across, 2))],
        compiler_params=pltpu.CompilerParams(vmem_limit_bytes=40 * 2**20),
        name="second",
    )(
        stay(depth), stay(bias_three), east1, north1, tracer1, feat, act, w1s, w2s, w3s, b1r, b2r,
        sel_in, sel_out,
    )
    return east[None], north[None], tracer[None]


def solution(mesh):
    field = P("group", "tile", None)
    in_specs = (field, field, field, P("tile", None)) + (P(),) * 7
    return jax.shard_map(
        body, mesh=mesh, in_specs=in_specs, out_specs=(field,) * 3, check_vma=False
    )
```

```python
import functools

import jax
import jax.numpy as jnp
from jax import lax
from jax.experimental import pallas as pl
from jax.experimental.pallas import tpu as pltpu
from jax.sharding import PartitionSpec as P

time_step = 0.1
viscosity = 0.5
diffusivity = 0.5
eddy_gain = 0.5
coriolis_base = 0.2
coriolis_slope = 0.6

bf16 = jnp.bfloat16
f32 = jnp.float32

TS = 128
HALO = 5
ROWS1, ROWS2 = 35, 34
SLAB = 160
USED = 144


def build_tables(sel_in, sel_out, pick):
    row = lax.broadcasted_iota(jnp.int32, (80, 256), 0)
    col = lax.broadcasted_iota(jnp.int32, (80, 256), 1)
    sel_in[...] = (col == 2 * (9 * (row % 8) + row // 8)).astype(f32).astype(bf16)
    row = lax.broadcasted_iota(jnp.int32, (USED, 256), 0)
    col = lax.broadcasted_iota(jnp.int32, (USED, 256), 1)
    place = 2 * (9 * (row % 8) + row // 16)
    inside = place + 1 < 130
    for ip in range(2):
        for b in range(2):
            hit = inside & ((row % 16) // 8 == ip) & (col == (place + b + 255) % 256)
            sel_out[ip, b] = hit.astype(f32).astype(bf16)
    row = lax.broadcasted_iota(jnp.int32, (16, TS), 0)
    col = lax.broadcasted_iota(jnp.int32, (16, TS), 1)
    pick[...] = (row == col).astype(f32).astype(bf16)


def taps():
    for outer in range(2):
        for inner in range(2):
            for out in range(2):
                k = 2 * outer + inner - out
                if 0 <= k < 3:
                    yield outer, inner, out, k


def build_weights(w1, w2, w3, b1, b2, w1f, w1s, w2s, w3f, w3s, b1r, b2r):
    w1f[...] = jnp.zeros_like(w1f)
    for c in range(3):
        for kx in range(3):
            line = 0.5 * w1[c, kx].astype(f32)
            for q in range(4):
                for dj, dy, b, ky in taps():
                    for a in range(2):
                        row = dj * 128 + dy * 48 + c * 16 + 4 + 2 * q + a + kx
                        lane = (a * 2 + b) * 64
                        w1f[q, row : row + 1, lane : lane + 64] = line[ky : ky + 1]
    w1s[...] = w1f[...].astype(bf16)
    w2s[...] = jnp.zeros_like(w2s)
    for kx in range(3):
        for ky in range(3):
            block = (0.5 * w2[kx, ky].astype(f32)).T.astype(bf16)
            for di, ai, ao, kx_here in taps():
                for dj, bi, bo, ky_here in taps():
                    if (kx, ky) == (kx_here, ky_here):
                        row = (ai * 2 + bi) * 64
                        lane = (ao * 2 + bo) * 64
                        w2s[di * 2 + dj, row : row + 64, lane : lane + 64] = block
    w3f[...] = jnp.zeros_like(w3f)
    for c in range(3):
        for kx in range(3):
            line = w3[c, kx].astype(f32)
            for di, ai, ao, kx_here in taps():
                if kx != kx_here:
                    continue
                for dj, bi, bo, ky in taps():
                    lane = (ai * 2 + bi) * 64
                    row = (di * 2 + dj) * 16 + bo * 6 + c * 2 + ao
                    w3f[row : row + 1, lane : lane + 64] = line[ky : ky + 1]
    turned = w3f[...].T.astype(bf16)
    row = lax.broadcasted_iota(jnp.int32, (64, 256), 0)
    col = lax.broadcasted_iota(jnp.int32, (64, 256), 1)
    part = row % 16
    di, dj = row // 32, (row // 16) % 2
    b, c, a = part // 6, (part % 6) // 2, part % 2
    for j in range(8):
        into = jnp.where(j - di >= 0, c * 16 + 2 * (j - di), 48 + 2 * c)
        hit = (part < 12) & (col == dj * 128 + b * 64 + into + a)
        spread = jnp.dot(turned, hit.astype(f32).astype(bf16), preferred_element_type=f32)
        w3s[256 * j : 256 * j + 256, :] = spread.astype(bf16)
    for j in range(4):
        b1r[:, 64 * j : 64 * j + 64] = 0.5 * b1[...]
        b2r[:, 64 * j : 64 * j + 64] = 0.5 * b2[...]


def wet_line(depth, level, tile_row, lane, across):
    line = jnp.zeros(lane.shape, f32)
    for ty in range(across):
        wet = (depth[tile_row * across + ty] > level).astype(f32)
        line = jnp.where(lane // TS == ty, wet, line)
    return line


def feature_rows(k, tile, rows_all, wet, ext, landx, east, north, tracer, feat, act, act0, store):
    cols = landx.shape[1]
    lane = lax.broadcasted_iota(jnp.int32, (8, cols), 1)
    row = lax.broadcasted_iota(jnp.int32, (8, cols), 0)
    zeros = jnp.zeros((8, TS), f32)

    def west(x):
        return jnp.where(lane == 0, 0.0, pltpu.roll(x, 1, 1))

    def east_of(x):
        return jnp.where(lane == cols - 1, 0.0, pltpu.roll(x, cols - 1, 1))

    base = 8 * k + 16
    water = jnp.where(landx[base : base + 8, :] == 1, 1.0, 0.0)
    active = water * wet
    mid = [ext[f, base : base + 8, :] for f in range(3)]
    up = [ext[f, base - 1 : base + 7, :] for f in range(3)]
    down = [ext[f, base + 1 : base + 9, :] for f in range(3)]
    left = [west(x) for x in mid]
    right = [east_of(x) for x in mid]
    lap = [down[f] + up[f] + right[f] + left[f] - 4.0 * mid[f] for f in range(3)]
    grad_east = 0.5 * (down[2] - up[2])
    grad_north = 0.5 * (right[2] - left[2])
    place = (tile * TS + 8 * k + row).astype(f32)
    coriolis = coriolis_base + coriolis_slope * (place + 0.5) / rows_all
    step = time_step * active
    new_east = mid[0] + step * (coriolis * mid[1] - grad_east + viscosity * lap[0])
    new_north = mid[1] + step * (-coriolis * mid[0] - grad_north + viscosity * lap[1])
    new_tracer = mid[2] + step * (
        -(mid[0] * grad_east + mid[1] * grad_north) + diffusivity * lap[2]
    )
    if store:
        at = 8 * k
        east[pl.ds(at, 8), :] = new_east
        north[pl.ds(at, 8), :] = new_north
        tracer[pl.ds(at, 8), :] = new_tracer
    q = 8 * k + 8
    for c, new in enumerate((new_east, new_north, new_tracer)):
        wide = jnp.concatenate([new * active, zeros], axis=1)
        feat[c, pl.ds(q, 8), :] = pltpu.roll(wide, 4, 1)
    act[pl.ds(q, 8), :] = pltpu.roll(jnp.concatenate([active, zeros], axis=1), 1, 1)
    act0[pl.ds(q, 8), :] = pltpu.roll(jnp.concatenate([water, zeros], axis=1), 1, 1)


def silu_half(half):
    return half + half * jnp.tanh(half)


def store_slab(ref, index, value):
    ref[index, 0:USED, :] = value.astype(bf16)
    ref[index, USED:SLAB, :] = pltpu.roll(value[0:16], 15, 0).astype(bf16)


def closure_pieces(tables, weights, work, b3, read_rows, read_mask, put):
    sel_in, sel_out = tables
    w1s, w2s, w3s, b1, b2 = weights
    patches, h1, h2, parts, flat, image = work

    def gather(g):
        halves = []
        for ip in range(2):
            rows = read_rows(64 * ip + 8 * g).reshape(48, 256)
            rows = jnp.concatenate([rows, pltpu.roll(rows, 255, 1), jnp.zeros((32, 256), f32)], axis=0)
            got = lax.dot_general(
                sel_in[...], rows.astype(bf16), (((1,), (1,)), ((), ())), preferred_element_type=f32
            )
            halves.append(got.reshape(10, 8, 128))
        both = jnp.stack(halves, axis=1).reshape(SLAB, 128).astype(bf16)
        patches[g, :, 0:128] = both[0:USED]
        patches[g, :, 128:256] = both[16:SLAB]

    def first(q, start):
        count = 3 if 4 * (start + 2) + q < ROWS1 else 2
        lhs = patches[start : start + count].reshape(count * USED, 256)
        half = jnp.dot(lhs, w1s[q], preferred_element_type=f32) + b1[...]
        out = silu_half(half)
        for g in range(count):
            store_slab(h1, 4 * (start + g) + q, out[g * USED : (g + 1) * USED])

    def second(i):
        half = b2[...]
        for di in range(2):
            for dj in range(2):
                lhs = h1[i + di : i + di + 2, 16 * dj : 16 * dj + USED, :].reshape(2 * USED, 256)
                half = half + jnp.dot(lhs, w2s[2 * di + dj], preferred_element_type=f32)
        out = silu_half(half).astype(bf16)
        m, j = i // 8, i % 8
        h2[m, :, 256 * j : 256 * j + 256] = out[0:USED]
        h2[m, :, 256 * j + 256 : 256 * j + 512] = out[USED:]

    def third(m):
        depth = 2048 if m < 4 else 512
        got = jnp.dot(h2[m, :, 0:depth], w3s[0:depth, :], preferred_element_type=f32)
        here, later = got[:, 0:128], got[:, 128:256]
        later = jnp.concatenate([later[16:USED], pltpu.roll(later[0:16], 15, 0)], axis=0)
        parts[m] = (here + later).T

    def settle(m):
        for b in range(2):
            for c in range(3):
                at = b * 64 + c * 16
                rows = parts[m, at : at + 16, :]
                if m < 4:
                    rest = parts[m + 1, b * 64 + 48 + 2 * c : b * 64 + 50 + 2 * c, :]
                    rows = rows + jnp.concatenate([jnp.zeros((14, USED), f32), rest], axis=0)
                flat[b, 48 * m + 16 * c : 48 * m + 16 * c + 16, :] = (rows + b3[c]).astype(bf16)

    def unfold(ip):
        rows = 192 + 48 * ip
        whole = jnp.dot(flat[0, 0:rows], sel_out[ip, 0], preferred_element_type=f32) + jnp.dot(
            flat[1, 0:rows], sel_out[ip, 1], preferred_element_type=f32
        )
        for m in range(4 + ip):
            for c in range(3):
                row = 64 * ip + 16 * m
                image[c, row : row + 16, :] = whole[48 * m + 16 * c : 48 * m + 16 * c + 16]

    def push():
        mask = pltpu.roll(read_mask(), 255, 1)
        xx, xy, yy = [image[c, 0:130, :] * mask for c in range(3)]

        def dx(m):
            return m[2:130, 0:TS] - m[0:128, 0:TS]

        def dy(m):
            mid = m[1:129]
            return pltpu.roll(mid, 255, 1)[:, 0:TS] - pltpu.roll(mid, 1, 1)[:, 0:TS]

        gain = (0.5 * eddy_gain) * mask[1:129, 0:TS]
        put(gain * (dx(xx) + dy(xy)), gain * (dx(xy) + dy(yy)))

    gathers = [functools.partial(gather, g) for g in range(9)]
    firsts = [functools.partial(first, q, start) for q in range(4) for start in range(0, 9, 3)]
    seconds = [functools.partial(second, i) for i in range(0, ROWS2, 2)]
    thirds = [functools.partial(third, m) for m in range(5)]
    rest = [functools.partial(settle, m) for m in range(5)]
    rest += [functools.partial(unfold, ip) for ip in range(2)] + [push]
    return gathers, firsts, seconds, thirds, rest


def run_all(*lists):
    for pieces in lists:
        for piece in pieces:
            piece()


def run_woven(gathers, firsts, seconds, thirds, rest):
    beside = {}
    for g, piece in enumerate(gathers):
        beside.setdefault(GATHER_AT[g], []).append(piece)
    for n, piece in enumerate(rest):
        beside.setdefault(REST_AT[n], []).append(piece)
    run_all(firsts)
    for i, piece in enumerate(seconds):
        piece()
        run_all(beside.get(i, []))
    run_all(thirds)


GATHER_AT = (7, 8, 9, 10, 11, 12, 13, 14, 15)
REST_AT = (0, 1, 2, 3, 4, 5, 6, 8)


KEPT = 5


def first_kernel(
    depth_h, b3_h, u, v, t, land, w1h, w2h, w3h, b1h, b2h,
    east, north, tracer, feat, act, w1s, w2s, w3s, b1r, b2r, sel_in, sel_out,
    depth, b3, ext, landx, act0, w1f, w3f, w1, w2, w3, b1, b2, pick,
    patches, h1, h2, parts, flat, image, win,
    main_out, edge_out, main_in, edge_in, res_out, res_in,
    load_sem, halo_send, halo_recv, win_send, win_recv, res_send, res_recv,
):
    level, tile = lax.axis_index("group"), lax.axis_index("tile")
    tiles = lax.axis_size("tile")
    cols = u.shape[1]
    across = cols // TS
    mesh_id = pl.DeviceIdType.MESH

    loads = [
        pltpu.make_async_copy(origin, place, load_sem.at[i])
        for i, (origin, place) in enumerate(
            (
                (w1h, w1),
                (w2h, w2),
                (w3h, w3),
                (b1h, b1),
                (b2h, b2),
                (b3_h, b3),
                (depth_h, depth),
                (u, ext.at[0, pl.ds(16, TS)]),
                (v, ext.at[1, pl.ds(16, TS)]),
                (t, ext.at[2, pl.ds(16, TS)]),
                (land, landx.at[pl.ds(16, TS)]),
            )
        )
    ]
    for load in loads:
        load.start()

    barrier = pltpu.get_barrier_semaphore()

    def greet(group, place):
        pl.semaphore_signal(barrier, inc=1, device_id=(group, place), device_id_type=mesh_id)

    @pl.when(tile > 0)
    def _():
        greet(level, tile - 1)

    @pl.when(tile < tiles - 1)
    def _():
        greet(level, tile + 1)

    @pl.when(level == 0)
    def _():
        greet(2, tile)
        greet(3, tile)

    @pl.when(level >= 2)
    def _():
        greet(0, tile)

    peers = jnp.where(tile > 0, 1, 0) + jnp.where(tile < tiles - 1, 1, 0)
    peers = peers + jnp.where(level == 0, 2, jnp.where(level == 1, 0, 1))

    for f in range(3):
        ext[f, 0:8, :] = jnp.zeros((8, cols), f32)
        ext[f, 152:160, :] = jnp.zeros((8, cols), f32)
    landx[0:8, :] = jnp.zeros((8, cols), jnp.int32)
    landx[152:160, :] = jnp.zeros((8, cols), jnp.int32)
    pl.semaphore_wait(barrier, peers)

    def halo_copy(way, f):
        src = (u, v, t, land)[f]
        rows_from, rows_to, place = ((TS - 8, 8, tile + 1), (0, 144, tile - 1))[way]
        dst = ext.at[f, pl.ds(rows_to, 8)] if f < 3 else landx.at[pl.ds(rows_to, 8)]
        return pltpu.make_async_remote_copy(
            src_ref=src.at[pl.ds(rows_from, 8)],
            dst_ref=dst,
            send_sem=halo_send.at[way, f],
            recv_sem=halo_recv.at[way, f],
            device_id=(level, place),
            device_id_type=mesh_id,
        )

    @pl.when(tile < tiles - 1)
    def _():
        for f in range(4):
            halo_copy(0, f).start()

    @pl.when(tile > 0)
    def _():
        for f in range(4):
            halo_copy(1, f).start()

    @pl.when(tile == 0)
    def _():
        for f in range(3):
            ext[f, 8:16, :] = jnp.zeros((8, cols), f32)
        landx[8:16, :] = jnp.zeros((8, cols), jnp.int32)

    @pl.when(tile == tiles - 1)
    def _():
        for f in range(3):
            ext[f, 144:152, :] = jnp.zeros((8, cols), f32)
        landx[144:152, :] = jnp.zeros((8, cols), jnp.int32)

    build_tables(sel_in, sel_out, pick)
    for load in loads[5:7]:
        load.wait()
    lane = lax.broadcasted_iota(jnp.int32, (8, cols), 1)
    rows_all = float(tiles * TS)
    wet_mid = wet_line(depth, level, tile, lane, across)
    wet_low = wet_line(depth, level, (tile + tiles - 1) % tiles, lane, across)
    wet_high = wet_line(depth, level, (tile + 1) % tiles, lane, across)

    def rows_of(k, wet, store):
        feature_rows(
            k, tile, rows_all, wet, ext, landx, east, north, tracer, feat, act, act0, store
        )

    for load in loads[7:]:
        load.wait()
    for k in range(1, 15):
        rows_of(k, wet_mid, True)

    def window_copy(slot, part):
        group, place = ((2, 0), (3, 0), (3, 1))[slot]
        if part == 3:
            src, dst = edge_out.at[slot], edge_in.at[place]
        else:
            rows = pl.ds(*((16, 112), (0, 16), (128, 16))[part])
            src, dst = main_out.at[slot, :, rows], main_in.at[place, :, rows]
        return pltpu.make_async_remote_copy(
            src_ref=src,
            dst_ref=dst,
            send_sem=win_send.at[slot, part],
            recv_sem=win_recv.at[place, part],
            device_id=(group, tile),
            device_id_type=mesh_id,
        )

    @pl.when(level == 0)
    def _():
        for slot in (1, 0, 2):
            lane0 = (KEPT + slot) * TS
            main_out[slot, :, 16:128] = feat[:, 16:128, lane0 : lane0 + TS].astype(bf16)
            window_copy(slot, 0).start()

    for load in loads[:5]:
        load.wait()
    build_weights(w1, w2, w3, b1, b2, w1f, w1s, w2s, w3f, w3s, b1r, b2r)


    @pl.when(tile > 0)
    def _():
        for f in range(4):
            halo_copy(0, f).wait_recv()

    @pl.when(tile < tiles - 1)
    def _():
        for f in range(4):
            halo_copy(1, f).wait_recv()

    rows_of(-1, wet_low, False)
    rows_of(0, wet_mid, True)
    rows_of(15, wet_mid, True)
    rows_of(16, wet_high, False)

    @pl.when(level == 0)
    def _():
        for slot in (1, 0, 2):
            lane0 = (KEPT + slot) * TS
            for part, rows in ((1, slice(0, 16)), (2, slice(128, 144))):
                main_out[slot, :, rows] = feat[:, rows, lane0 : lane0 + TS].astype(bf16)
                window_copy(slot, part).start()
            edge = feat[:, :, lane0 + TS : lane0 + 2 * TS].reshape(432, TS).astype(bf16)
            edge_out[slot] = lax.dot_general(
                pick[...], edge, (((1,), (1,)), ((), ())), preferred_element_type=f32
            ).astype(bf16)
            window_copy(slot, 3).start()


    def result_copy(item):
        return pltpu.make_async_remote_copy(
            src_ref=res_out.at[item],
            dst_ref=res_in.at[level - 2 + item],
            send_sem=res_send.at[item],
            recv_sem=res_recv.at[level - 2 + item],
            device_id=(0, tile),
            device_id_type=mesh_id,
        )

    tables, weights = (sel_in, sel_out), (w1s, w2s, w3s, b1r, b2r)
    work = (patches, h1, h2, parts, flat, image)

    def own_pieces(next_item, last_item):
        next_lane = pl.multiple_of(next_item * TS, TS)
        last_lane = pl.multiple_of(jnp.where(last_item < 0, 0, last_item) * TS, TS)

        def put(push_east, push_north):
            for ref, push in ((east, push_east), (north, push_north)):
                ref[:, pl.ds(last_lane, TS)] += jnp.where(last_item < 0, 0.0, push)

        return closure_pieces(
            tables, weights, work, b3,
            lambda base: feat[:, pl.ds(base, 16), pl.ds(next_lane, 2 * TS)],
            lambda: act[7:137, pl.ds(last_lane, 2 * TS)],
            put,
        )

    @pl.when(level == 0)
    def _():
        parts[...] = jnp.zeros_like(parts)
        run_all(own_pieces(0, 0)[0])

        def item_step(item, carry):
            run_woven(*own_pieces(item + 1, item - 1))
            return carry

        lax.fori_loop(0, KEPT, item_step, 0)
        run_all(own_pieces(0, KEPT - 1)[4])

    @pl.when(level >= 2)
    def _():
        def item_step(item, carry):
            for part in range(4):
                if part == 3:
                    src, dst = edge_out.at[0], edge_in.at[item]
                else:
                    rows = pl.ds(*((16, 112), (0, 16), (128, 16))[part])
                    src, dst = main_out.at[0, :, rows], main_in.at[item, :, rows]
                pltpu.make_async_remote_copy(
                    src_ref=src,
                    dst_ref=dst,
                    send_sem=win_send.at[0, part],
                    recv_sem=win_recv.at[item, part],
                    device_id=(0, tile),
                    device_id_type=mesh_id,
                ).wait_recv()
            win[:, :, 0:TS] = main_in[item].astype(f32)
            edge = lax.dot_general(
                edge_in[item], pick[...], (((0,), (0,)), ((), ())), preferred_element_type=f32
            )
            win[:, :, TS : 2 * TS] = edge.reshape(3, 144, TS)
            from0 = pl.multiple_of((KEPT + level - 2 + item) * TS, TS)

            def put(push_east, push_north):
                res_out[item, 0] = push_east.astype(bf16)
                res_out[item, 1] = push_north.astype(bf16)

            run_all(
                *closure_pieces(
                    tables, weights, work, b3,
                    lambda base: win[:, base : base + 16, :],
                    lambda: act0[7:137, pl.ds(from0, 2 * TS)],
                    put,
                )
            )
            result_copy(item).start()
            return carry

        lax.fori_loop(0, level - 1, item_step, 0)

    @pl.when(level == 0)
    def _():
        for slot in range(3):
            pltpu.make_async_remote_copy(
                src_ref=res_out.at[0],
                dst_ref=res_in.at[slot],
                send_sem=res_send.at[0],
                recv_sem=res_recv.at[slot],
                device_id=(3, tile),
                device_id_type=mesh_id,
            ).wait_recv()
            lane0 = (KEPT + slot) * TS
            east[:, lane0 : lane0 + TS] += res_in[slot, 0].astype(f32)
            north[:, lane0 : lane0 + TS] += res_in[slot, 1].astype(f32)
            for part in range(4):
                window_copy(slot, part).wait_send()

    @pl.when(level == 2)
    def _():
        result_copy(0).wait_send()

    @pl.when(level == 3)
    def _():
        result_copy(0).wait_send()
        result_copy(1).wait_send()

    @pl.when(tile < tiles - 1)
    def _():
        for f in range(4):
            halo_copy(0, f).wait_send()

    @pl.when(tile > 0)
    def _():
        for f in range(4):
            halo_copy(1, f).wait_send()


def second_kernel(
    depth_h, b3_h, east1, north1, tracer1, feat, act, w1s, w2s, w3s, b1, b2, sel_in, sel_out,
    east, north, tracer,
    depth, b3, columns, sums, patches, h1, h2, parts, flat, image,
    load_sem, tracer_sem, out_sem,
):
    level, tile = lax.axis_index("group"), lax.axis_index("tile")
    across = east1.shape[1] // TS
    tracer_copy = pltpu.make_async_copy(tracer1, tracer, tracer_sem)
    loads = [
        pltpu.make_async_copy(b3_h, b3, load_sem.at[0]),
        pltpu.make_async_copy(depth_h, depth, load_sem.at[1]),
    ]
    for load in loads:
        load.start()
    tracer_copy.start()

    def block_copy(ty, which, source):
        lanes = pl.ds(pl.multiple_of(ty * TS, TS), TS)
        return pltpu.make_async_copy(
            source.at[:, lanes], (east, north)[which].at[:, lanes], out_sem.at[ty, which]
        )

    def whole_copy(which):
        return pltpu.make_async_copy(
            (east1, north1)[which], (east, north)[which], out_sem.at[0, which]
        )

    def send(ty):
        for which in range(2):
            block_copy(ty, which, sums.at[which]).start()

    @pl.when(level == 0)
    def _():
        for which in range(2):
            whole_copy(which).start()
        for load in loads:
            load.wait()
        for which in range(2):
            whole_copy(which).wait()

    @pl.when(level > 0)
    def _():
        for load in loads:
            load.wait()
        count = jnp.int32(0)
        for ty in range(across):
            mine = depth[tile * across + ty] > level
            columns[count] = jnp.int32(ty)
            count = count + mine.astype(jnp.int32)

            @pl.when(jnp.logical_not(mine))
            def _():
                for which in range(2):
                    block_copy(ty, which, (east1, north1)[which]).start()

        def own_pieces(next_item, last_item):
            next_lane = pl.multiple_of(columns[next_item] * TS, TS)
            last_lane = pl.multiple_of(columns[jnp.maximum(last_item, 0)] * TS, TS)

            def put(push_east, push_north):
                for which, push in ((0, push_east), (1, push_north)):
                    old = (east1, north1)[which][:, pl.ds(last_lane, TS)]
                    sums[which, :, pl.ds(last_lane, TS)] = old + jnp.where(last_item < 0, 0.0, push)

            return closure_pieces(
                (sel_in, sel_out), (w1s, w2s, w3s, b1, b2), (patches, h1, h2, parts, flat, image), b3,
                lambda base: feat[:, pl.ds(base, 16), pl.ds(next_lane, 2 * TS)],
                lambda: act[7:137, pl.ds(last_lane, 2 * TS)],
                put,
            )

        @pl.when(count > 0)
        def _():
            parts[...] = jnp.zeros_like(parts)
            run_all(own_pieces(0, 0)[0])

            def item_step(item, carry):
                run_woven(*own_pieces(jnp.minimum(item + 1, count - 1), item - 1))

                @pl.when(item > 0)
                def _():
                    send(columns[item - 1])

                return carry

            lax.fori_loop(0, count, item_step, 0)
            run_all(own_pieces(0, count - 1)[4])
            send(columns[count - 1])

        for ty in range(across):
            for which in range(2):
                block_copy(ty, which, sums.at[which]).wait()

    tracer_copy.wait()


def body(u, v, t, land, depth, conv_one, bias_one, conv_two, bias_two, conv_three, bias_three):
    levels, rows, cols = u.shape
    vmem = pl.BlockSpec(memory_space=pltpu.VMEM)
    hbm = pl.BlockSpec(memory_space=pltpu.HBM)
    wide = cols + TS
    across = cols // TS
    plane = jax.ShapeDtypeStruct((rows, cols), f32)
    work = [
        pltpu.VMEM((9, USED, 256), bf16),
        pltpu.VMEM((ROWS1 + 1, SLAB, 256), bf16),
        pltpu.VMEM((5, USED, 2048), bf16),
        pltpu.VMEM((5, TS, USED), f32),
        pltpu.VMEM((2, 240, USED), bf16),
        pltpu.VMEM((3, 144, 256), f32),
    ]
    def stay(x):
        return pltpu.with_memory_space_constraint(x, pltpu.HBM)

    east1, north1, tracer1, feat, act, w1s, w2s, w3s, b1r, b2r, sel_in, sel_out = pl.pallas_call(
        first_kernel,
        out_shape=[plane] * 3
        + [
            jax.ShapeDtypeStruct((3, 144, wide), f32),
            jax.ShapeDtypeStruct((144, wide), f32),
            jax.ShapeDtypeStruct((4, 256, 256), bf16),
            jax.ShapeDtypeStruct((4, 256, 256), bf16),
            jax.ShapeDtypeStruct((2048, 256), bf16),
            jax.ShapeDtypeStruct((1, 256), f32),
            jax.ShapeDtypeStruct((1, 256), f32),
            jax.ShapeDtypeStruct((80, 256), bf16),
            jax.ShapeDtypeStruct((2, 2, USED, 256), bf16),
        ],
        in_specs=[hbm] * 11,
        out_specs=[vmem] * 12,
        scratch_shapes=[
            pltpu.SMEM(depth.shape, jnp.int32),
            pltpu.SMEM((3,), f32),
            pltpu.VMEM((3, 160, cols), f32),
            pltpu.VMEM((160, cols), jnp.int32),
            pltpu.VMEM((144, wide), f32),
            pltpu.VMEM((4, 256, 256), f32),
            pltpu.VMEM((64, 256), f32),
            pltpu.VMEM((3, 3, 3, 64), bf16),
            pltpu.VMEM((3, 3, 64, 64), bf16),
            pltpu.VMEM((3, 3, 3, 64), bf16),
            pltpu.VMEM((1, 64), f32),
            pltpu.VMEM((1, 64), f32),
            pltpu.VMEM((16, TS), bf16),
        ]
        + work
        + [
            pltpu.VMEM((3, 144, 2 * TS), f32),
            pltpu.VMEM((3, 3, 144, TS), bf16),
            pltpu.VMEM((3, 16, 432), bf16),
            pltpu.VMEM((2, 3, 144, TS), bf16),
            pltpu.VMEM((2, 16, 432), bf16),
            pltpu.VMEM((2, 2, TS, TS), bf16),
            pltpu.VMEM((3, 2, TS, TS), bf16),
            pltpu.SemaphoreType.DMA((11,)),
            pltpu.SemaphoreType.DMA((2, 4)),
            pltpu.SemaphoreType.DMA((2, 4)),
            pltpu.SemaphoreType.DMA((3, 4)),
            pltpu.SemaphoreType.DMA((2, 4)),
            pltpu.SemaphoreType.DMA((2,)),
            pltpu.SemaphoreType.DMA((3,)),
        ],
        compiler_params=pltpu.CompilerParams(
            vmem_limit_bytes=40 * 2**20, collective_id=0, has_side_effects=True
        ),
        name="first",
    )(
        stay(depth), stay(bias_three), stay(u[0]), stay(v[0]), stay(t[0]), stay(land),
        stay(conv_one.transpose(1, 2, 3, 0)), stay(conv_two.transpose(2, 3, 0, 1)),
        stay(conv_three.transpose(0, 2, 3, 1)), stay(bias_one[None]), stay(bias_two[None]),
    )
    east, north, tracer = pl.pallas_call(
        second_kernel,
        out_shape=[plane] * 3,
        in_specs=[hbm] * 2 + [vmem] * 12,
        out_specs=[hbm] * 3,
        scratch_shapes=[
            pltpu.SMEM(depth.shape, jnp.int32),
            pltpu.SMEM((3,), f32),
            pltpu.SMEM((across,), jnp.int32),
            pltpu.VMEM((2, rows, cols), f32),
        ]
        + work
        + [pltpu.SemaphoreType.DMA((2,)), pltpu.SemaphoreType.DMA, pltpu.SemaphoreType.DMA((across, 2))],
        compiler_params=pltpu.CompilerParams(vmem_limit_bytes=40 * 2**20),
        name="second",
    )(
        stay(depth), stay(bias_three), east1, north1, tracer1, feat, act, w1s, w2s, w3s, b1r, b2r,
        sel_in, sel_out,
    )
    return east[None], north[None], tracer[None]


def solution(mesh):
    field = P("group", "tile", None)
    in_specs = (field, field, field, P("tile", None)) + (P(),) * 7
    return jax.shard_map(
        body, mesh=mesh, in_specs=in_specs, out_specs=(field,) * 3, check_vma=False
    )
```

```python
import functools

import jax
import jax.numpy as jnp
from jax import lax
from jax.experimental import pallas as pl
from jax.experimental.pallas import tpu as pltpu
from jax.sharding import PartitionSpec as P

time_step = 0.1
viscosity = 0.5
diffusivity = 0.5
eddy_gain = 0.5
coriolis_base = 0.2
coriolis_slope = 0.6

bf16 = jnp.bfloat16
f32 = jnp.float32

TS = 128
HALO = 5
ROWS1, ROWS2 = 35, 34
SLAB = 160
USED = 144


def build_tables(sel_in, sel_out, pick):
    row = lax.broadcasted_iota(jnp.int32, (80, 256), 0)
    col = lax.broadcasted_iota(jnp.int32, (80, 256), 1)
    sel_in[...] = (col == 2 * (9 * (row % 8) + row // 8)).astype(f32).astype(bf16)
    row = lax.broadcasted_iota(jnp.int32, (USED, 256), 0)
    col = lax.broadcasted_iota(jnp.int32, (USED, 256), 1)
    place = 2 * (9 * (row % 8) + row // 16)
    inside = place + 1 < 130
    for ip in range(2):
        for b in range(2):
            hit = inside & ((row % 16) // 8 == ip) & (col == (place + b + 255) % 256)
            sel_out[ip, b] = hit.astype(f32).astype(bf16)
    row = lax.broadcasted_iota(jnp.int32, (16, TS), 0)
    col = lax.broadcasted_iota(jnp.int32, (16, TS), 1)
    pick[...] = (row == col).astype(f32).astype(bf16)


def taps():
    for outer in range(2):
        for inner in range(2):
            for out in range(2):
                k = 2 * outer + inner - out
                if 0 <= k < 3:
                    yield outer, inner, out, k


def build_weights(w1, w2, w3, b1, b2, w1f, w1s, w2s, w3f, w3s, b1r, b2r):
    w1f[...] = jnp.zeros_like(w1f)
    for c in range(3):
        for kx in range(3):
            line = 0.5 * w1[c, kx].astype(f32)
            for q in range(4):
                for dj, dy, b, ky in taps():
                    for a in range(2):
                        row = dj * 128 + dy * 48 + c * 16 + 4 + 2 * q + a + kx
                        lane = (a * 2 + b) * 64
                        w1f[q, row : row + 1, lane : lane + 64] = line[ky : ky + 1]
    w1s[...] = w1f[...].astype(bf16)
    w2s[...] = jnp.zeros_like(w2s)
    for kx in range(3):
        for ky in range(3):
            block = (0.5 * w2[kx, ky].astype(f32)).T.astype(bf16)
            for di, ai, ao, kx_here in taps():
                for dj, bi, bo, ky_here in taps():
                    if (kx, ky) == (kx_here, ky_here):
                        row = (ai * 2 + bi) * 64
                        lane = (ao * 2 + bo) * 64
                        w2s[di * 2 + dj, row : row + 64, lane : lane + 64] = block
    w3f[...] = jnp.zeros_like(w3f)
    for c in range(3):
        for kx in range(3):
            line = w3[c, kx].astype(f32)
            for di, ai, ao, kx_here in taps():
                if kx != kx_here:
                    continue
                for dj, bi, bo, ky in taps():
                    lane = (ai * 2 + bi) * 64
                    row = (di * 2 + dj) * 16 + bo * 6 + c * 2 + ao
                    w3f[row : row + 1, lane : lane + 64] = line[ky : ky + 1]
    turned = w3f[...].T.astype(bf16)
    row = lax.broadcasted_iota(jnp.int32, (64, 256), 0)
    col = lax.broadcasted_iota(jnp.int32, (64, 256), 1)
    part = row % 16
    di, dj = row // 32, (row // 16) % 2
    b, c, a = part // 6, (part % 6) // 2, part % 2
    for j in range(8):
        into = jnp.where(j - di >= 0, c * 16 + 2 * (j - di), 48 + 2 * c)
        hit = (part < 12) & (col == dj * 128 + b * 64 + into + a)
        spread = jnp.dot(turned, hit.astype(f32).astype(bf16), preferred_element_type=f32)
        w3s[256 * j : 256 * j + 256, :] = spread.astype(bf16)
    for j in range(4):
        b1r[:, 64 * j : 64 * j + 64] = 0.5 * b1[...]
        b2r[:, 64 * j : 64 * j + 64] = 0.5 * b2[...]


def wet_line(depth, level, tile_row, lane, across):
    line = jnp.zeros(lane.shape, f32)
    for ty in range(across):
        wet = (depth[tile_row * across + ty] > level).astype(f32)
        line = jnp.where(lane // TS == ty, wet, line)
    return line


def feature_rows(k, tile, rows_all, wet, ext, landx, east, north, tracer, feat, act, store):
    cols = landx.shape[1]
    lane = lax.broadcasted_iota(jnp.int32, (8, cols), 1)
    row = lax.broadcasted_iota(jnp.int32, (8, cols), 0)
    zeros = jnp.zeros((8, TS), f32)

    def west(x):
        return jnp.where(lane == 0, 0.0, pltpu.roll(x, 1, 1))

    def east_of(x):
        return jnp.where(lane == cols - 1, 0.0, pltpu.roll(x, cols - 1, 1))

    base = 8 * k + 16
    water = jnp.where(landx[base : base + 8, :] == 1, 1.0, 0.0)
    active = water * wet
    mid = [ext[f, base : base + 8, :] for f in range(3)]
    up = [ext[f, base - 1 : base + 7, :] for f in range(3)]
    down = [ext[f, base + 1 : base + 9, :] for f in range(3)]
    left = [west(x) for x in mid]
    right = [east_of(x) for x in mid]
    lap = [down[f] + up[f] + right[f] + left[f] - 4.0 * mid[f] for f in range(3)]
    grad_east = 0.5 * (down[2] - up[2])
    grad_north = 0.5 * (right[2] - left[2])
    place = (tile * TS + 8 * k + row).astype(f32)
    coriolis = coriolis_base + coriolis_slope * (place + 0.5) / rows_all
    step = time_step * active
    new_east = mid[0] + step * (coriolis * mid[1] - grad_east + viscosity * lap[0])
    new_north = mid[1] + step * (-coriolis * mid[0] - grad_north + viscosity * lap[1])
    new_tracer = mid[2] + step * (
        -(mid[0] * grad_east + mid[1] * grad_north) + diffusivity * lap[2]
    )
    if store:
        at = 8 * k
        east[pl.ds(at, 8), :] = new_east
        north[pl.ds(at, 8), :] = new_north
        tracer[pl.ds(at, 8), :] = new_tracer
    q = 8 * k + 8
    for c, new in enumerate((new_east, new_north, new_tracer)):
        wide = jnp.concatenate([new * active, zeros], axis=1)
        feat[c, pl.ds(q, 8), :] = pltpu.roll(wide, 4, 1)
    act[pl.ds(q, 8), :] = pltpu.roll(jnp.concatenate([active, zeros], axis=1), 1, 1)


def silu_half(half):
    return half + half * jnp.tanh(half)


def store_slab(ref, index, value):
    ref[index, 0:USED, :] = value.astype(bf16)
    ref[index, USED:SLAB, :] = pltpu.roll(value[0:16], 15, 0).astype(bf16)


def closure_pieces(tables, weights, work, b3, read_rows, read_mask, put):
    sel_in, sel_out = tables
    w1s, w2s, w3s, b1, b2 = weights
    patches, h1, h2, parts, flat, image = work

    def gather(g):
        halves = []
        for ip in range(2):
            rows = read_rows(64 * ip + 8 * g).reshape(48, 256)
            rows = jnp.concatenate([rows, pltpu.roll(rows, 255, 1)], axis=0)
            got = lax.dot_general(
                sel_in[...], rows.astype(bf16), (((1,), (1,)), ((), ())), preferred_element_type=f32
            )
            halves.append(got.reshape(10, 8, 96))
        both = jnp.stack(halves, axis=1).reshape(SLAB, 96).astype(bf16)
        patches[g, :, 0:96] = both[0:USED]
        patches[g, :, 128:224] = both[16:SLAB]

    def first(q, start):
        count = 3 if 4 * (start + 2) + q < ROWS1 else 2
        lhs = patches[start : start + count].reshape(count * USED, 256)
        half = jnp.dot(lhs, w1s[q], preferred_element_type=f32) + b1[...]
        out = silu_half(half)
        for g in range(count):
            store_slab(h1, 4 * (start + g) + q, out[g * USED : (g + 1) * USED])

    def second(i):
        half = b2[...]
        for di in range(2):
            for dj in range(2):
                lhs = h1[i + di : i + di + 2, 16 * dj : 16 * dj + USED, :].reshape(2 * USED, 256)
                half = half + jnp.dot(lhs, w2s[2 * di + dj], preferred_element_type=f32)
        out = silu_half(half).astype(bf16)
        m, j = i // 8, i % 8
        h2[m, :, 256 * j : 256 * j + 256] = out[0:USED]
        h2[m, :, 256 * j + 256 : 256 * j + 512] = out[USED:]

    def third(m):
        depth = 2048 if m < 4 else 512
        got = jnp.dot(h2[m, :, 0:depth], w3s[0:depth, :], preferred_element_type=f32)
        here, later = got[:, 0:128], got[:, 128:256]
        later = jnp.concatenate([later[16:USED], pltpu.roll(later[0:16], 15, 0)], axis=0)
        parts[m] = (here + later).T

    def settle(m):
        for b in range(2):
            for c in range(3):
                at = b * 64 + c * 16
                rows = parts[m, at : at + 16, :]
                if m < 4:
                    rest = parts[m + 1, b * 64 + 48 + 2 * c : b * 64 + 50 + 2 * c, :]
                    rows = rows + jnp.concatenate([jnp.zeros((14, USED), f32), rest], axis=0)
                flat[b, 48 * m + 16 * c : 48 * m + 16 * c + 16, :] = (rows + b3[c]).astype(bf16)

    def unfold(ip):
        rows = 192 + 48 * ip
        whole = jnp.dot(flat[0, 0:rows], sel_out[ip, 0], preferred_element_type=f32) + jnp.dot(
            flat[1, 0:rows], sel_out[ip, 1], preferred_element_type=f32
        )
        for m in range(4 + ip):
            for c in range(3):
                row = 64 * ip + 16 * m
                image[c, row : row + 16, :] = whole[48 * m + 16 * c : 48 * m + 16 * c + 16]

    def push():
        mask = pltpu.roll(read_mask(), 255, 1)
        xx, xy, yy = [image[c, 0:130, :] * mask for c in range(3)]

        def dx(m):
            return m[2:130, 0:TS] - m[0:128, 0:TS]

        def dy(m):
            mid = m[1:129]
            return pltpu.roll(mid, 255, 1)[:, 0:TS] - pltpu.roll(mid, 1, 1)[:, 0:TS]

        gain = (0.5 * eddy_gain) * mask[1:129, 0:TS]
        put(gain * (dx(xx) + dy(xy)), gain * (dx(xy) + dy(yy)))

    gathers = [functools.partial(gather, g) for g in range(9)]
    firsts = [functools.partial(first, q, start) for q in range(4) for start in range(0, 9, 3)]
    seconds = [functools.partial(second, i) for i in range(0, ROWS2, 2)]
    thirds = [functools.partial(third, m) for m in range(5)]
    rest = [functools.partial(settle, m) for m in range(5)]
    rest += [functools.partial(unfold, ip) for ip in range(2)] + [push]
    return gathers, firsts, seconds, thirds, rest


def run_all(*lists):
    for pieces in lists:
        for piece in pieces:
            piece()


def run_woven(gathers, firsts, seconds, thirds, rest):
    beside = {}
    for g, piece in enumerate(gathers):
        beside.setdefault(GATHER_AT[g], []).append(piece)
    for n, piece in enumerate(rest):
        beside.setdefault(REST_AT[n], []).append(piece)
    run_all(firsts)
    for i, piece in enumerate(seconds):
        piece()
        run_all(beside.get(i, []))
    run_all(thirds)


GATHER_AT = (7, 8, 9, 10, 11, 12, 13, 14, 15)
REST_AT = (0, 1, 2, 3, 4, 5, 6, 8)


KEPT = 5


def first_kernel(
    depth_h, b3_h, u, v, t, land, w1h, w2h, w3h, b1h, b2h,
    east, north, tracer, feat, act, w1s, w2s, w3s, b1r, b2r, sel_in, sel_out,
    depth, b3, ext, landx, act0, w1f, w3f, w1, w2, w3, b1, b2, pick,
    patches, h1, h2, parts, flat, image, win,
    main_out, edge_out, main_in, edge_in, res_out, res_in,
    load_sem, halo_send, halo_recv, win_send, win_recv, res_send, res_recv,
):
    level, tile = lax.axis_index("group"), lax.axis_index("tile")
    tiles = lax.axis_size("tile")
    cols = u.shape[1]
    across = cols // TS
    mesh_id = pl.DeviceIdType.MESH

    loads = [
        pltpu.make_async_copy(origin, place, load_sem.at[i])
        for i, (origin, place) in enumerate(
            (
                (w1h, w1),
                (w2h, w2),
                (w3h, w3),
                (b1h, b1),
                (b2h, b2),
                (b3_h, b3),
                (depth_h, depth),
                (u, ext.at[0, pl.ds(16, TS)]),
                (v, ext.at[1, pl.ds(16, TS)]),
                (t, ext.at[2, pl.ds(16, TS)]),
                (land, landx.at[pl.ds(16, TS)]),
            )
        )
    ]
    for load in loads:
        load.start()

    barrier = pltpu.get_barrier_semaphore()

    def greet(group, place):
        pl.semaphore_signal(barrier, inc=1, device_id=(group, place), device_id_type=mesh_id)

    @pl.when(tile > 0)
    def _():
        greet(level, tile - 1)

    @pl.when(tile < tiles - 1)
    def _():
        greet(level, tile + 1)

    @pl.when(level == 0)
    def _():
        greet(2, tile)
        greet(3, tile)

    @pl.when(level >= 2)
    def _():
        greet(0, tile)

    peers = jnp.where(tile > 0, 1, 0) + jnp.where(tile < tiles - 1, 1, 0)
    peers = peers + jnp.where(level == 0, 2, jnp.where(level == 1, 0, 1))

    for f in range(3):
        ext[f, 0:8, :] = jnp.zeros((8, cols), f32)
        ext[f, 152:160, :] = jnp.zeros((8, cols), f32)
    landx[0:8, :] = jnp.zeros((8, cols), jnp.int32)
    landx[152:160, :] = jnp.zeros((8, cols), jnp.int32)
    pl.semaphore_wait(barrier, peers)

    def halo_copy(way, f):
        src = (u, v, t, land)[f]
        rows_from, rows_to, place = ((TS - 8, 8, tile + 1), (0, 144, tile - 1))[way]
        dst = ext.at[f, pl.ds(rows_to, 8)] if f < 3 else landx.at[pl.ds(rows_to, 8)]
        return pltpu.make_async_remote_copy(
            src_ref=src.at[pl.ds(rows_from, 8)],
            dst_ref=dst,
            send_sem=halo_send.at[way, f],
            recv_sem=halo_recv.at[way, f],
            device_id=(level, place),
            device_id_type=mesh_id,
        )

    @pl.when(tile < tiles - 1)
    def _():
        for f in range(4):
            halo_copy(0, f).start()

    @pl.when(tile > 0)
    def _():
        for f in range(4):
            halo_copy(1, f).start()

    @pl.when(tile == 0)
    def _():
        for f in range(3):
            ext[f, 8:16, :] = jnp.zeros((8, cols), f32)
        landx[8:16, :] = jnp.zeros((8, cols), jnp.int32)

    @pl.when(tile == tiles - 1)
    def _():
        for f in range(3):
            ext[f, 144:152, :] = jnp.zeros((8, cols), f32)
        landx[144:152, :] = jnp.zeros((8, cols), jnp.int32)

    build_tables(sel_in, sel_out, pick)
    patches[...] = jnp.zeros_like(patches)
    for load in loads[5:7]:
        load.wait()
    lane = lax.broadcasted_iota(jnp.int32, (8, cols), 1)
    rows_all = float(tiles * TS)
    wet_mid = wet_line(depth, level, tile, lane, across)
    wet_low = wet_line(depth, level, (tile + tiles - 1) % tiles, lane, across)
    wet_high = wet_line(depth, level, (tile + 1) % tiles, lane, across)

    def rows_of(k, wet, store):
        feature_rows(
            k, tile, rows_all, wet, ext, landx, east, north, tracer, feat, act, store
        )

    for load in loads[7:]:
        load.wait()
    for k in range(1, 15):
        rows_of(k, wet_mid, True)

    def window_copy(slot, part):
        group, place = ((2, 0), (3, 0), (3, 1))[slot]
        if part == 3:
            src, dst = edge_out.at[slot], edge_in.at[place]
        else:
            rows = pl.ds(*((16, 112), (0, 16), (128, 16))[part])
            src, dst = main_out.at[slot, :, rows], main_in.at[place, :, rows]
        return pltpu.make_async_remote_copy(
            src_ref=src,
            dst_ref=dst,
            send_sem=win_send.at[slot, part],
            recv_sem=win_recv.at[place, part],
            device_id=(group, tile),
            device_id_type=mesh_id,
        )

    @pl.when(level == 0)
    def _():
        for slot in (1, 0, 2):
            lane0 = (KEPT + slot) * TS
            main_out[slot, :, 16:128] = feat[:, 16:128, lane0 : lane0 + TS].astype(bf16)
            window_copy(slot, 0).start()

    for load in loads[:5]:
        load.wait()
    build_weights(w1, w2, w3, b1, b2, w1f, w1s, w2s, w3f, w3s, b1r, b2r)


    @pl.when(tile > 0)
    def _():
        for f in range(4):
            halo_copy(0, f).wait_recv()

    @pl.when(tile < tiles - 1)
    def _():
        for f in range(4):
            halo_copy(1, f).wait_recv()

    rows_of(-1, wet_low, False)
    rows_of(0, wet_mid, True)
    rows_of(15, wet_mid, True)
    rows_of(16, wet_high, False)

    @pl.when(level == 0)
    def _():
        for slot in (1, 0, 2):
            lane0 = (KEPT + slot) * TS
            for part, rows in ((1, slice(0, 16)), (2, slice(128, 144))):
                main_out[slot, :, rows] = feat[:, rows, lane0 : lane0 + TS].astype(bf16)
                window_copy(slot, part).start()
            edge = feat[:, :, lane0 + TS : lane0 + 2 * TS].reshape(432, TS).astype(bf16)
            edge_out[slot] = lax.dot_general(
                pick[...], edge, (((1,), (1,)), ((), ())), preferred_element_type=f32
            ).astype(bf16)
            window_copy(slot, 3).start()


    def result_copy(item):
        return pltpu.make_async_remote_copy(
            src_ref=res_out.at[item],
            dst_ref=res_in.at[level - 2 + item],
            send_sem=res_send.at[item],
            recv_sem=res_recv.at[level - 2 + item],
            device_id=(0, tile),
            device_id_type=mesh_id,
        )

    tables, weights = (sel_in, sel_out), (w1s, w2s, w3s, b1r, b2r)
    work = (patches, h1, h2, parts, flat, image)

    def own_pieces(next_item, last_item):
        next_lane = pl.multiple_of(next_item * TS, TS)
        last_lane = pl.multiple_of(jnp.where(last_item < 0, 0, last_item) * TS, TS)

        def put(push_east, push_north):
            for ref, push in ((east, push_east), (north, push_north)):
                ref[:, pl.ds(last_lane, TS)] += jnp.where(last_item < 0, 0.0, push)

        return closure_pieces(
            tables, weights, work, b3,
            lambda base: feat[:, pl.ds(base, 16), pl.ds(next_lane, 2 * TS)],
            lambda: act[7:137, pl.ds(last_lane, 2 * TS)],
            put,
        )

    @pl.when(level == 0)
    def _():
        parts[...] = jnp.zeros_like(parts)
        run_all(own_pieces(0, 0)[0])

        def item_step(item, carry):
            run_woven(*own_pieces(item + 1, item - 1))
            return carry

        lax.fori_loop(0, KEPT, item_step, 0)
        run_all(own_pieces(0, KEPT - 1)[4])

    @pl.when(level >= 2)
    def _():
        for k in range(-1, 17):
            water = jnp.where(landx[8 * k + 16 : 8 * k + 24, :] == 1, 1.0, 0.0)
            wide_water = jnp.concatenate([water, jnp.zeros((8, TS), f32)], axis=1)
            act0[8 * k + 8 : 8 * k + 16, :] = pltpu.roll(wide_water, 1, 1)

        def item_step(item, carry):
            for part in range(4):
                if part == 3:
                    src, dst = edge_out.at[0], edge_in.at[item]
                else:
                    rows = pl.ds(*((16, 112), (0, 16), (128, 16))[part])
                    src, dst = main_out.at[0, :, rows], main_in.at[item, :, rows]
                pltpu.make_async_remote_copy(
                    src_ref=src,
                    dst_ref=dst,
                    send_sem=win_send.at[0, part],
                    recv_sem=win_recv.at[item, part],
                    device_id=(0, tile),
                    device_id_type=mesh_id,
                ).wait_recv()
            win[:, :, 0:TS] = main_in[item].astype(f32)
            edge = lax.dot_general(
                edge_in[item], pick[...], (((0,), (0,)), ((), ())), preferred_element_type=f32
            )
            win[:, :, TS : 2 * TS] = edge.reshape(3, 144, TS)
            from0 = pl.multiple_of((KEPT + level - 2 + item) * TS, TS)

            def put(push_east, push_north):
                res_out[item, 0] = push_east.astype(bf16)
                res_out[item, 1] = push_north.astype(bf16)

            run_all(
                *closure_pieces(
                    tables, weights, work, b3,
                    lambda base: win[:, base : base + 16, :],
                    lambda: act0[7:137, pl.ds(from0, 2 * TS)],
                    put,
                )
            )
            result_copy(item).start()
            return carry

        lax.fori_loop(0, level - 1, item_step, 0)

    @pl.when(level == 0)
    def _():
        for slot in range(3):
            pltpu.make_async_remote_copy(
                src_ref=res_out.at[0],
                dst_ref=res_in.at[slot],
                send_sem=res_send.at[0],
                recv_sem=res_recv.at[slot],
                device_id=(3, tile),
                device_id_type=mesh_id,
            ).wait_recv()
            lane0 = (KEPT + slot) * TS
            east[:, lane0 : lane0 + TS] += res_in[slot, 0].astype(f32)
            north[:, lane0 : lane0 + TS] += res_in[slot, 1].astype(f32)
            for part in range(4):
                window_copy(slot, part).wait_send()

    @pl.when(level == 2)
    def _():
        result_copy(0).wait_send()

    @pl.when(level == 3)
    def _():
        result_copy(0).wait_send()
        result_copy(1).wait_send()

    @pl.when(tile < tiles - 1)
    def _():
        for f in range(4):
            halo_copy(0, f).wait_send()

    @pl.when(tile > 0)
    def _():
        for f in range(4):
            halo_copy(1, f).wait_send()


def second_kernel(
    depth_h, b3_h, east1, north1, tracer1, feat, act, w1s, w2s, w3s, b1, b2, sel_in, sel_out,
    east, north, tracer,
    depth, b3, columns, sums, patches, h1, h2, parts, flat, image,
    load_sem, tracer_sem, out_sem,
):
    level, tile = lax.axis_index("group"), lax.axis_index("tile")
    across = east1.shape[1] // TS
    tracer_copy = pltpu.make_async_copy(tracer1, tracer, tracer_sem)
    loads = [
        pltpu.make_async_copy(b3_h, b3, load_sem.at[0]),
        pltpu.make_async_copy(depth_h, depth, load_sem.at[1]),
    ]
    for load in loads:
        load.start()
    tracer_copy.start()

    def block_copy(ty, which, source):
        lanes = pl.ds(pl.multiple_of(ty * TS, TS), TS)
        return pltpu.make_async_copy(
            source.at[:, lanes], (east, north)[which].at[:, lanes], out_sem.at[ty, which]
        )

    def whole_copy(which):
        return pltpu.make_async_copy(
            (east1, north1)[which], (east, north)[which], out_sem.at[0, which]
        )

    def send(ty):
        for which in range(2):
            block_copy(ty, which, sums.at[which]).start()

    @pl.when(level == 0)
    def _():
        for which in range(2):
            whole_copy(which).start()
        for load in loads:
            load.wait()
        for which in range(2):
            whole_copy(which).wait()

    @pl.when(level > 0)
    def _():
        for load in loads:
            load.wait()
        count = jnp.int32(0)
        for ty in range(across):
            mine = depth[tile * across + ty] > level
            columns[count] = jnp.int32(ty)
            count = count + mine.astype(jnp.int32)

            @pl.when(jnp.logical_not(mine))
            def _():
                for which in range(2):
                    block_copy(ty, which, (east1, north1)[which]).start()

        def own_pieces(next_item, last_item):
            next_lane = pl.multiple_of(columns[next_item] * TS, TS)
            last_lane = pl.multiple_of(columns[jnp.maximum(last_item, 0)] * TS, TS)

            def put(push_east, push_north):
                for which, push in ((0, push_east), (1, push_north)):
                    old = (east1, north1)[which][:, pl.ds(last_lane, TS)]
                    sums[which, :, pl.ds(last_lane, TS)] = old + jnp.where(last_item < 0, 0.0, push)

            return closure_pieces(
                (sel_in, sel_out), (w1s, w2s, w3s, b1, b2), (patches, h1, h2, parts, flat, image), b3,
                lambda base: feat[:, pl.ds(base, 16), pl.ds(next_lane, 2 * TS)],
                lambda: act[7:137, pl.ds(last_lane, 2 * TS)],
                put,
            )

        @pl.when(count > 0)
        def _():
            parts[...] = jnp.zeros_like(parts)
            patches[...] = jnp.zeros_like(patches)
            run_all(own_pieces(0, 0)[0])

            def item_step(item, carry):
                run_woven(*own_pieces(jnp.minimum(item + 1, count - 1), item - 1))

                @pl.when(item > 0)
                def _():
                    send(columns[item - 1])

                return carry

            lax.fori_loop(0, count, item_step, 0)
            run_all(own_pieces(0, count - 1)[4])
            send(columns[count - 1])

        for ty in range(across):
            for which in range(2):
                block_copy(ty, which, sums.at[which]).wait()

    tracer_copy.wait()


def body(u, v, t, land, depth, conv_one, bias_one, conv_two, bias_two, conv_three, bias_three):
    levels, rows, cols = u.shape
    vmem = pl.BlockSpec(memory_space=pltpu.VMEM)
    hbm = pl.BlockSpec(memory_space=pltpu.HBM)
    wide = cols + TS
    across = cols // TS
    plane = jax.ShapeDtypeStruct((rows, cols), f32)
    work = [
        pltpu.VMEM((9, USED, 256), bf16),
        pltpu.VMEM((ROWS1 + 1, SLAB, 256), bf16),
        pltpu.VMEM((5, USED, 2048), bf16),
        pltpu.VMEM((5, TS, USED), f32),
        pltpu.VMEM((2, 240, USED), bf16),
        pltpu.VMEM((3, 144, 256), f32),
    ]
    def stay(x):
        return pltpu.with_memory_space_constraint(x, pltpu.HBM)

    east1, north1, tracer1, feat, act, w1s, w2s, w3s, b1r, b2r, sel_in, sel_out = pl.pallas_call(
        first_kernel,
        out_shape=[plane] * 3
        + [
            jax.ShapeDtypeStruct((3, 144, wide), f32),
            jax.ShapeDtypeStruct((144, wide), f32),
            jax.ShapeDtypeStruct((4, 256, 256), bf16),
            jax.ShapeDtypeStruct((4, 256, 256), bf16),
            jax.ShapeDtypeStruct((2048, 256), bf16),
            jax.ShapeDtypeStruct((1, 256), f32),
            jax.ShapeDtypeStruct((1, 256), f32),
            jax.ShapeDtypeStruct((80, 256), bf16),
            jax.ShapeDtypeStruct((2, 2, USED, 256), bf16),
        ],
        in_specs=[hbm] * 11,
        out_specs=[vmem] * 12,
        scratch_shapes=[
            pltpu.SMEM(depth.shape, jnp.int32),
            pltpu.SMEM((3,), f32),
            pltpu.VMEM((3, 160, cols), f32),
            pltpu.VMEM((160, cols), jnp.int32),
            pltpu.VMEM((144, wide), f32),
            pltpu.VMEM((4, 256, 256), f32),
            pltpu.VMEM((64, 256), f32),
            pltpu.VMEM((3, 3, 3, 64), bf16),
            pltpu.VMEM((3, 3, 64, 64), bf16),
            pltpu.VMEM((3, 3, 3, 64), bf16),
            pltpu.VMEM((1, 64), f32),
            pltpu.VMEM((1, 64), f32),
            pltpu.VMEM((16, TS), bf16),
        ]
        + work
        + [
            pltpu.VMEM((3, 144, 2 * TS), f32),
            pltpu.VMEM((3, 3, 144, TS), bf16),
            pltpu.VMEM((3, 16, 432), bf16),
            pltpu.VMEM((2, 3, 144, TS), bf16),
            pltpu.VMEM((2, 16, 432), bf16),
            pltpu.VMEM((2, 2, TS, TS), bf16),
            pltpu.VMEM((3, 2, TS, TS), bf16),
            pltpu.SemaphoreType.DMA((11,)),
            pltpu.SemaphoreType.DMA((2, 4)),
            pltpu.SemaphoreType.DMA((2, 4)),
            pltpu.SemaphoreType.DMA((3, 4)),
            pltpu.SemaphoreType.DMA((2, 4)),
            pltpu.SemaphoreType.DMA((2,)),
            pltpu.SemaphoreType.DMA((3,)),
        ],
        compiler_params=pltpu.CompilerParams(
            vmem_limit_bytes=40 * 2**20, collective_id=0, has_side_effects=True
        ),
        name="first",
    )(
        stay(depth), stay(bias_three), stay(u[0]), stay(v[0]), stay(t[0]), stay(land),
        stay(conv_one.transpose(1, 2, 3, 0)), stay(conv_two.transpose(2, 3, 0, 1)),
        stay(conv_three.transpose(0, 2, 3, 1)), stay(bias_one[None]), stay(bias_two[None]),
    )
    east, north, tracer = pl.pallas_call(
        second_kernel,
        out_shape=[plane] * 3,
        in_specs=[hbm] * 2 + [vmem] * 12,
        out_specs=[hbm] * 3,
        scratch_shapes=[
            pltpu.SMEM(depth.shape, jnp.int32),
            pltpu.SMEM((3,), f32),
            pltpu.SMEM((across,), jnp.int32),
            pltpu.VMEM((2, rows, cols), f32),
        ]
        + work
        + [pltpu.SemaphoreType.DMA((2,)), pltpu.SemaphoreType.DMA, pltpu.SemaphoreType.DMA((across, 2))],
        compiler_params=pltpu.CompilerParams(vmem_limit_bytes=40 * 2**20),
        name="second",
    )(
        stay(depth), stay(bias_three), east1, north1, tracer1, feat, act, w1s, w2s, w3s, b1r, b2r,
        sel_in, sel_out,
    )
    return east[None], north[None], tracer[None]


def solution(mesh):
    field = P("group", "tile", None)
    in_specs = (field, field, field, P("tile", None)) + (P(),) * 7
    return jax.shard_map(
        body, mesh=mesh, in_specs=in_specs, out_specs=(field,) * 3, check_vma=False
    )
```
